256 devices in a mesh: dom: 128 (over y, x, z), grp: 2 (over core).
Axes of the slice: x: 4, y: 4, z: 8, core: 2. Of those that a mesh axis runs over, the one named last changes fastest.
Arguments:
- features: bfloat16 [65536, 512], P(('dom', 'grp')), may hold values from -6 to 6
- hub_feat: bfloat16 [2048, 512], P(('dom', 'grp')), may hold values from -6 to 6
- adjacency: bfloat16 [6144, 128, 128], P(('dom', 'grp')), may hold values from 0 to 1
- block_row: int32 [256, 24], P(('dom', 'grp')), may hold values from 0 to 1
- block_col: int32 [256, 24], P(('dom', 'grp')), may hold values from 0 to 18
- block_count: int32 [256], P(('dom', 'grp')), may hold values from 18 to 24, as said below
- halo_send: int32 [256, 128], P(('dom', 'grp')), may hold values from 0 to 255
- w_self: bfloat16 [512, 512], replicated, may hold values from -0.25 to 0.25
- w_neigh: bfloat16 [512, 512], replicated, may hold values from -0.25 to 0.25
- out_grad: bfloat16 [65536, 512], P(('dom', 'grp')), may hold values from -6 to 6
Outputs:
- activations: bfloat16 [65536, 512], P(('dom', 'grp'))
- grad_features: float32 [65536, 512], P(('dom', 'grp'))
- grad_hub: float32 [2048, 512], P(('dom', 'grp'))
- grad_w_self: float32 [512, 512], replicated
- grad_w_neigh: float32 [512, 512], replicated
The draws below stay inside these ranges and needn't reach their ends.
Inputs may be any that keep to these rules, and one draw needn't show every extreme that they name: `block_count`: slots at or past a partition's count are padding and are ignored; some partition uses all 24 slots.
All inputs are finite; a program needn't handle non-finite values.
Results may differ from the reference program's by a relative error of at most 0.015.
Values may be sent and summed in bfloat16 or wider, within the bound.
No kernel may reach another device: no remote copies, remote signals or barrier semaphores. Data moves between devices by JAX's collectives and lax.ppermute only.
A program may use at most 64 MiB of HBM per device.

```python
import math
import jax
import jax.numpy as jnp
from jax import lax

D = 512
TILE = 128
ROW_BLOCKS = 2
LOCAL_ROWS = 256
BLOCKS = 24
HUBS = 2048
NODES = 65536
COL_BLOCKS = 19
N_DOM = 128
N_GRP = 2
DEVICES = 256


def draw_block_count(key, part):
    key = jax.random.fold_in(key, 11)
    base_key, pick_key = jax.random.split(key, 2)
    lowest = BLOCKS * 3 // 4
    counts = lowest + jax.random.randint(base_key, (DEVICES,), 0, BLOCKS - lowest + 1, dtype=jnp.int32)
    chosen = jax.random.randint(pick_key, (), 0, DEVICES, dtype=jnp.int32)
    return counts.at[chosen].set(BLOCKS).astype(jnp.int32)


def draw_block_col(key, part):
    key = jax.random.fold_in(key, 23)
    coin_key, hub_key, local_key = jax.random.split(key, 3)
    coin = jax.random.randint(coin_key, (DEVICES, BLOCKS), 0, 2, dtype=jnp.int32)
    hub_pick = jax.random.randint(hub_key, (DEVICES, BLOCKS), ROW_BLOCKS + 1, COL_BLOCKS, dtype=jnp.int32)
    local_pick = jax.random.randint(local_key, (DEVICES, BLOCKS), 0, ROW_BLOCKS + 1, dtype=jnp.int32)
    return jnp.where(coin == 1, hub_pick, local_pick).astype(jnp.int32)


def touch_ends(values, stream_key, low, top_value):
    longest = values.shape.index(max(values.shape))
    spots = []
    for shift in (0, 1):
        where = [jax.random.randint(jax.random.fold_in(stream_key, axis), (), 0, length) for axis, length in enumerate(values.shape)]
        where[longest] = (where[longest] + shift) % values.shape[longest]
        spots.append(tuple(where))
    return values.at[spots[0]].set(low).at[spots[1]].set(top_value)


def block_levels(stream_key, extent, cuts, low, largest):
    def one(axis_at, shards_of):
        draws = jax.random.uniform(jax.random.fold_in(jax.random.fold_in(stream_key, 6), axis_at), (shards_of,), jnp.float32, low / len(cuts), largest / len(cuts))
        return jnp.repeat(jnp.exp(draws), extent[axis_at] // shards_of).reshape((-1,) + (1,) * (len(extent) - axis_at - 1))

    gain = one(*cuts[0])
    for cut in cuts[1:]:
        gain = gain * one(*cut)
    return gain


def gaussian(rng, shape, spread, reach, cuts=(), held_as=jnp.bfloat16):
    level = block_levels(rng, shape, cuts, -0.22, 0.18) if cuts else 1.0
    result = jax.random.normal(rng, shape, jnp.float32) * spread * level
    return jnp.minimum(jnp.maximum(result, -reach), reach).astype(held_as)


def setup_inputs(seed: int = 0) -> dict:
    key_of = jax.random.split(jax.random.key(seed), 11)
    features = gaussian(key_of[0], (NODES, D), 1.0, 6.0, ((0, 256),))
    hub_feat = gaussian(key_of[1], (HUBS, D), 1.0, 6.0, ((0, 256),))
    adjacency = jnp.clip(1.0 * jax.random.uniform(key_of[2], (DEVICES * BLOCKS, TILE, TILE), jnp.float32) ** block_levels(key_of[2], (DEVICES * BLOCKS, TILE, TILE), ((0, 256),), -0.2, 0.2), 0.0, 1.0).astype(jnp.bfloat16)
    block_row = touch_ends(jax.random.randint(key_of[3], (DEVICES, BLOCKS), 0, ROW_BLOCKS), jax.random.fold_in(key_of[3], 1), 0, ROW_BLOCKS - 1).astype(jnp.int32)
    block_col = draw_block_col(jax.random.fold_in(key_of[10], 71), 0)
    block_count = draw_block_count(jax.random.fold_in(key_of[10], 71), 0)
    halo_send = touch_ends(jax.random.randint(key_of[6], (DEVICES, TILE), 0, LOCAL_ROWS), jax.random.fold_in(key_of[6], 1), 0, LOCAL_ROWS - 1).astype(jnp.int32)
    w_self = gaussian(key_of[7], (D, D), D ** -0.5, 0.25)
    w_neigh = gaussian(key_of[8], (D, D), D ** -0.5, 0.25)
    out_grad = gaussian(key_of[9], (NODES, D), 1.0, 6.0, ((0, 256),))
    return {"features": features, "hub_feat": hub_feat, "adjacency": adjacency, "block_row": block_row, "block_col": block_col, "block_count": block_count, "halo_send": halo_send, "w_self": w_self, "w_neigh": w_neigh, "out_grad": out_grad}


def partition_pass(own_rows, halo_in, hub_table, tile_set, rows_index, cols_index, used_count, grad_out, w_self, w_neigh):
    usable = jnp.arange(BLOCKS, dtype=jnp.int32) < used_count
    sources = jnp.concatenate([own_rows, halo_in, hub_table], 0).reshape(COL_BLOCKS, TILE, D)
    picked = sources[cols_index]
    tiles_wide = tile_set.astype(jnp.float32)
    products = jnp.einsum('nij,njd->nid', tiles_wide, picked.astype(jnp.float32))
    row_onehot = jnp.where((rows_index[None, :] == jnp.arange(ROW_BLOCKS, dtype=jnp.int32)[:, None]) & usable[None, :], 1.0, 0.0).astype(jnp.float32)
    summed = jnp.einsum('rn,nid->rid', row_onehot, products).reshape(LOCAL_ROWS, D)
    degree = jnp.einsum('rn,ni->ri', row_onehot, lax.optimization_barrier(jnp.sum(tiles_wide, axis=2))).reshape(LOCAL_ROWS)
    norm_scale = (1.0 / jnp.sqrt(1.0 + degree))[:, None]
    aggregate = (summed * norm_scale).astype(jnp.bfloat16)
    preact = jnp.dot(own_rows, w_self, preferred_element_type=jnp.float32) + jnp.dot(aggregate, w_neigh, preferred_element_type=jnp.float32)
    activ = jax.nn.silu(preact).astype(jnp.bfloat16)
    sigmoid_val = jax.nn.sigmoid(preact)
    grad_pre = (grad_out.astype(jnp.float32) * sigmoid_val * (1.0 + preact * (1.0 - sigmoid_val))).astype(jnp.bfloat16)
    grad_self_w = jnp.dot(own_rows.T, grad_pre, preferred_element_type=jnp.float32)
    grad_neigh_w = jnp.dot(aggregate.T, grad_pre, preferred_element_type=jnp.float32)
    grad_input = jnp.dot(grad_pre, w_self.T, preferred_element_type=jnp.float32)
    grad_agg = (jnp.dot(grad_pre, w_neigh.T, preferred_element_type=jnp.float32) * norm_scale).astype(jnp.bfloat16)
    grad_blocks = grad_agg.reshape(ROW_BLOCKS, TILE, D)[rows_index]
    grad_products = jnp.einsum('nji,njd->nid', tiles_wide, grad_blocks.astype(jnp.float32))
    col_onehot = jnp.where((cols_index[None, :] == jnp.arange(COL_BLOCKS, dtype=jnp.int32)[:, None]) & usable[None, :], 1.0, 0.0).astype(jnp.float32)
    grad_sources = jnp.einsum('cn,nid->cid', col_onehot, grad_products).reshape(COL_BLOCKS * TILE, D)
    own_grad = grad_input + grad_sources[:LOCAL_ROWS]
    halo_grad = grad_sources[LOCAL_ROWS:LOCAL_ROWS + TILE]
    hub_grad = grad_sources[LOCAL_ROWS + TILE:]
    return (activ, own_grad, halo_grad, hub_grad, grad_self_w, grad_neigh_w)

def reference(features, hub_feat, adjacency, block_row, block_col, block_count, halo_send, w_self, w_neigh, out_grad):
    parts = N_DOM * N_GRP
    own_all = features.reshape(parts, LOCAL_ROWS, D)
    grad_all = out_grad.reshape(parts, LOCAL_ROWS, D)
    outgoing = jax.vmap(lambda rows_in, picks: rows_in[picks])(own_all, halo_send)
    halo_in = jnp.roll(outgoing.reshape(N_DOM, N_GRP, TILE, D), 1, axis=0).reshape(parts, TILE, D)
    tile_sets = adjacency.reshape(parts, BLOCKS, TILE, TILE)

    def step(carry, items):
        total_self, total_neigh, total_hub = carry
        own_rows, halo_rows, tile_set, rows_index, cols_index, used_count, grad_out = items
        activ, own_grad, halo_grad, hub_grad, grad_self_w, grad_neigh_w = partition_pass(own_rows, halo_rows, hub_feat, tile_set, rows_index, cols_index, used_count, grad_out, w_self, w_neigh)
        return ((total_self + grad_self_w, total_neigh + grad_neigh_w, total_hub + hub_grad), (activ, own_grad, halo_grad))
    start = (jnp.zeros((D, D), jnp.float32), jnp.zeros((D, D), jnp.float32), jnp.zeros((HUBS, D), jnp.float32))
    totals, outputs = lax.scan(step, start, (own_all, halo_in, tile_sets, block_row, block_col, block_count, grad_all))
    total_self, total_neigh, grad_hub = totals
    activ, own_grad, halo_grad = outputs
    returned = jnp.roll(halo_grad.reshape(N_DOM, N_GRP, TILE, D), -1, axis=0).reshape(parts, TILE, D)
    grad_features = jax.vmap(lambda base, picks, extra: base.at[picks].add(extra))(own_grad, halo_send, returned)
    factor = 1.0 / math.sqrt(NODES)
    return (activ.reshape(NODES, D), grad_features.reshape(NODES, D), grad_hub, total_self * factor, total_neigh * factor)
```

```python
import math

import jax
import jax.numpy as jnp
from jax import lax
from jax.sharding import Mesh
from jax.sharding import PartitionSpec as P

D = 512
BLOCKS_PER_ROW = 12
ALL = ("y", "x", "z", "c")
PLANE = ("y", "x")


def swap_cores(value):
    return lax.ppermute(value, "c", [(0, 1), (1, 0)])


def ring_shift(value, steps):
    count = 1
    for axis in ("y", "x", "z"):
        count *= lax.axis_size(axis)
    pairs = [(source, (source + steps) % count) for source in range(count)]
    return lax.ppermute(value, ("y", "x", "z"), pairs)


def exchange(value, axes):
    return lax.all_to_all(value, axes, 0, 0, tiled=True)


def spread(value, axes, count):
    return exchange(jnp.broadcast_to(value[None], (count,) + value.shape), axes)


def gather_hubs(hub_feat, zs, planes):
    core = lax.axis_index("c")
    column = spread(hub_feat, "z", zs)
    mine = spread(column, PLANE, planes)
    other = swap_cores(mine)
    low = jnp.where(core == 0, mine, other)
    high = jnp.where(core == 0, other, mine)
    return jnp.stack([low, high], 2).reshape(-1, D)


def reduce_all(hub_partial, self_partial, neigh_partial, zs, planes):
    core = lax.axis_index("c")
    hubs = hub_partial.astype(jnp.bfloat16).reshape(planes, zs, 2, -1, D)
    hubs = jnp.transpose(hubs, (2, 0, 1, 3, 4)).reshape(2, planes, -1, D)
    weights = jnp.stack([self_partial, neigh_partial]).astype(jnp.bfloat16)
    weights = weights.reshape(2, planes, -1, D)
    both = jnp.concatenate([hubs, weights], 2)
    mine = jnp.where(core == 0, both[0], both[1])
    theirs = jnp.where(core == 0, both[1], both[0])
    got = swap_cores(theirs)
    chip = (mine.astype(jnp.float32) + got.astype(jnp.float32)).astype(jnp.bfloat16)
    plane = jnp.sum(exchange(chip, PLANE).astype(jnp.float32), 0).astype(jnp.bfloat16)
    hub_rows = hubs.shape[2]
    hub_part = plane[:hub_rows].reshape(zs, -1, D)
    weight_part = plane[hub_rows:]
    packed = jnp.concatenate(
        [hub_part, jnp.broadcast_to(weight_part[None], (zs,) + weight_part.shape)], 1
    )
    total = jnp.sum(exchange(packed, "z").astype(jnp.float32), 0)
    own = hub_part.shape[1]
    weight_mine = spread(total[own:].astype(jnp.bfloat16), PLANE, planes).reshape(-1, D)
    weight_other = swap_cores(weight_mine)
    total_self = jnp.where(core == 0, weight_mine, weight_other).astype(jnp.float32)
    total_neigh = jnp.where(core == 0, weight_other, weight_mine).astype(jnp.float32)
    return total[:own], total_self, total_neigh


def per_device(
    features,
    hub_feat,
    adjacency,
    block_row,
    block_col,
    block_count,
    halo_send,
    w_self,
    w_neigh,
    out_grad,
):
    zs = lax.axis_size("z")
    planes = lax.axis_size("y") * lax.axis_size("x")
    local_rows = features.shape[0]
    tile_size = adjacency.shape[1]
    row_blocks = local_rows // tile_size
    slot_total = adjacency.shape[0]
    group_slots = BLOCKS_PER_ROW
    group_count = slot_total // group_slots
    rows_index = block_row[0]
    cols_index = block_col[0]
    send_rows = halo_send[0]
    usable = jnp.arange(slot_total, dtype=jnp.int32) < block_count[0]
    outgoing = features[send_rows]
    halo_rows = ring_shift(outgoing, 1)
    hub_table = gather_hubs(hub_feat, zs, planes)
    sources = jnp.concatenate([features, halo_rows, hub_table], 0).reshape(-1, tile_size, D)
    col_blocks = sources.shape[0]
    row_onehot = jnp.where(
        (rows_index[None, :] == jnp.arange(row_blocks, dtype=jnp.int32)[:, None]) & usable[None, :],
        1.0,
        0.0,
    ).astype(jnp.float32)
    col_onehot = jnp.where(
        (cols_index[None, :] == jnp.arange(col_blocks, dtype=jnp.int32)[:, None]) & usable[None, :],
        1.0,
        0.0,
    ).astype(jnp.float32)
    tile_groups = adjacency.reshape(group_count, group_slots, tile_size, tile_size)
    row_groups = rows_index.reshape(group_count, group_slots)
    col_groups = cols_index.reshape(group_count, group_slots)
    row_masks = jnp.transpose(row_onehot.reshape(row_blocks, group_count, group_slots), (1, 0, 2))
    col_masks = jnp.transpose(col_onehot.reshape(col_blocks, group_count, group_slots), (1, 0, 2))

    def forward_group(total, items):
        tiles, cols_here, mask_here = items
        picked = sources[cols_here]
        products = jnp.einsum("nij,njd->nid", tiles, picked, preferred_element_type=jnp.float32)
        return (total + jnp.einsum("rn,nid->rid", mask_here, products), None)

    summed, _ = lax.scan(
        forward_group,
        jnp.zeros((row_blocks, tile_size, D), jnp.float32),
        (tile_groups, col_groups, row_masks),
    )
    summed = summed.reshape(local_rows, D)
    row_weights = jnp.sum(adjacency, axis=2, dtype=jnp.float32)
    degree = jnp.einsum("rn,ni->ri", row_onehot, row_weights).reshape(local_rows)
    norm_scale = (1.0 / jnp.sqrt(1.0 + degree))[:, None]
    aggregate = (summed * norm_scale).astype(jnp.bfloat16)
    preact = jnp.dot(features, w_self, preferred_element_type=jnp.float32) + jnp.dot(
        aggregate, w_neigh, preferred_element_type=jnp.float32
    )
    activations = jax.nn.silu(preact).astype(jnp.bfloat16)
    sigmoid_val = jax.nn.sigmoid(preact)
    grad_pre = (
        out_grad.astype(jnp.float32) * sigmoid_val * (1.0 + preact * (1.0 - sigmoid_val))
    ).astype(jnp.bfloat16)
    lead_dims = (((0,), (0,)), ((), ()))
    grad_self_w = lax.dot_general(features, grad_pre, lead_dims, preferred_element_type=jnp.float32)
    grad_neigh_w = lax.dot_general(
        aggregate, grad_pre, lead_dims, preferred_element_type=jnp.float32
    )
    factor = 1.0 / math.sqrt(local_rows * 2 * zs * planes)
    trail_dims = (((1,), (1,)), ((), ()))
    grad_input = lax.dot_general(grad_pre, w_self, trail_dims, preferred_element_type=jnp.float32)
    grad_agg = (
        lax.dot_general(grad_pre, w_neigh, trail_dims, preferred_element_type=jnp.float32)
        * norm_scale
    ).astype(jnp.bfloat16)
    grad_tiles = grad_agg.reshape(row_blocks, tile_size, D)

    def backward_group(total, items):
        tiles, rows_here, mask_here = items
        grad_blocks = grad_tiles[rows_here]
        grad_products = jnp.einsum(
            "nji,njd->nid", tiles, grad_blocks, preferred_element_type=jnp.float32
        )
        return (total + jnp.einsum("cn,nid->cid", mask_here, grad_products), None)

    grad_sources, _ = lax.scan(
        backward_group,
        jnp.zeros((col_blocks, tile_size, D), jnp.float32),
        (tile_groups, row_groups, col_masks),
    )
    grad_sources = grad_sources.reshape(-1, D)
    halo_grad = grad_sources[local_rows : local_rows + tile_size]
    hub_partial = grad_sources[local_rows + tile_size :]
    returned = ring_shift(halo_grad.astype(jnp.bfloat16), -1).astype(halo_grad.dtype)
    grad_hub, total_self, total_neigh = reduce_all(
        hub_partial, grad_self_w, grad_neigh_w, zs, planes
    )
    grad_features = (grad_input + grad_sources[:local_rows]).at[send_rows].add(returned)
    return (activations, grad_features, grad_hub, total_self * factor, total_neigh * factor)


def solution(mesh):
    inner = Mesh(mesh.devices.reshape(4, 4, 8, 2), ALL)
    in_specs = (
        P(ALL, None),
        P(ALL, None),
        P(ALL, None, None),
        P(ALL, None),
        P(ALL, None),
        P(ALL),
        P(ALL, None),
        P(),
        P(),
        P(ALL, None),
    )
    out_specs = (
        P(ALL, None),
        P(ALL, None),
        P(ALL, None),
        P(),
        P(),
    )
    return jax.shard_map(
        per_device, mesh=inner, in_specs=in_specs, out_specs=out_specs, check_vma=False
    )
```

```python
import functools
import math

import jax
import jax.numpy as jnp
from jax import lax
from jax.experimental import pallas as pl
from jax.experimental.pallas import tpu as pltpu
from jax.sharding import Mesh
from jax.sharding import PartitionSpec as P

D = 512
TILE = 128
ROW_BLOCKS = 2
LOCAL_ROWS = ROW_BLOCKS * TILE
OWN = 8
F32 = jnp.float32
BF16 = jnp.bfloat16
ALL = ("y", "x", "z", "c")
PLANE = ("y", "x")


def dot(a, b, contract=((1,), (0,))):
    return lax.dot_general(a, b, (contract, ((), ())), preferred_element_type=F32)


def layer_kernel(
    count_ref,
    row_ref,
    col_ref,
    core_ref,
    feat_ref,
    halo_ref,
    mine_ref,
    other_ref,
    adj_ref,
    ws_ref,
    wn_ref,
    og_ref,
    act_ref,
    base_ref,
    back_ref,
    keep_ref,
    send_ref,
    table,
    wide,
    wide_t,
    gathered,
    acc,
):
    slots = adj_ref.shape[0]
    hub_tiles, column_rows, _ = mine_ref.shape
    first_hub = ROW_BLOCKS + 1
    count = count_ref[0]
    low_core = core_ref[0] == 0
    weight_rows = D // hub_tiles

    table[:LOCAL_ROWS] = feat_ref[...]
    table[LOCAL_ROWS : LOCAL_ROWS + TILE] = halo_ref[...]

    def fill(t, carry):
        here = mine_ref[t].astype(F32)
        there = other_ref[t].astype(F32)
        low = jnp.where(low_core, here, there)
        high = jnp.where(low_core, there, here)
        pieces = []
        for at in range(0, column_rows, OWN):
            pieces += [low[at : at + OWN], high[at : at + OWN]]
        start = pl.multiple_of((first_hub + t) * TILE, TILE)
        table[pl.ds(start, TILE)] = jnp.concatenate(pieces, 0).astype(BF16)
        return carry

    lax.fori_loop(0, hub_tiles, fill, 0)

    for s in range(slots):
        span = pl.ds(s * TILE, TILE)
        tile = adj_ref[s]
        flipped = tile.T
        blank = jnp.zeros_like(tile)
        for r in range(ROW_BLOCKS):
            on = (row_ref[0, s] == r) & (s < count)
            wide[r * TILE : (r + 1) * TILE, span] = jnp.where(on, tile, blank)
            wide_t[span, r * TILE : (r + 1) * TILE] = jnp.where(on, flipped, blank)
        start = pl.multiple_of(col_ref[0, s] * TILE, TILE)
        gathered[span] = table[pl.ds(start, TILE)]

    degree = dot(wide[...], jnp.ones((slots * TILE, TILE), BF16))
    norm = 1.0 / jnp.sqrt(1.0 + degree)
    norm = jnp.concatenate([norm] * (D // TILE), 1)
    summed = dot(wide[...], gathered[...])
    aggregate = (summed * norm).astype(BF16)
    own = feat_ref[...]
    preact = dot(own, ws_ref[...]) + dot(aggregate, wn_ref[...])
    gate = jax.nn.sigmoid(preact)
    act_ref[...] = (preact * gate).astype(BF16)
    grad_pre = (og_ref[...].astype(F32) * gate * (1.0 + preact * (1.0 - gate))).astype(BF16)
    grad_agg = (dot(grad_pre, wn_ref[...], ((1,), (1,))) * norm).astype(BF16)

    acc[...] = jnp.zeros_like(acc)
    for s in range(slots):
        into = pl.ds(pl.multiple_of(col_ref[0, s] * TILE, TILE), TILE)
        acc[into] += dot(wide_t[s * TILE : (s + 1) * TILE], grad_agg)

    def ship(t, carry):
        start = pl.multiple_of((first_hub + t) * TILE, TILE)
        grads = acc[pl.ds(start, TILE)]
        low = jnp.concatenate([grads[at : at + OWN] for at in range(0, TILE, 2 * OWN)], 0)
        high = jnp.concatenate([grads[at + OWN : at + 2 * OWN] for at in range(0, TILE, 2 * OWN)], 0)
        keep_ref[t, :column_rows] = jnp.where(low_core, low, high).astype(BF16)
        send_ref[t, :column_rows] = jnp.where(low_core, high, low).astype(BF16)
        return carry

    lax.fori_loop(0, hub_tiles, ship, 0)

    grad_self_w = dot(own, grad_pre, ((0,), (0,)))
    grad_neigh_w = dot(aggregate, grad_pre, ((0,), (0,)))
    keep = jnp.where(low_core, grad_self_w, grad_neigh_w).astype(BF16)
    send = jnp.where(low_core, grad_neigh_w, grad_self_w).astype(BF16)
    keep_ref[:, column_rows:] = keep.reshape(hub_tiles, weight_rows, D)
    send_ref[:, column_rows:] = send.reshape(hub_tiles, weight_rows, D)
    base_ref[...] = dot(grad_pre, ws_ref[...], ((1,), (1,))) + acc[:LOCAL_ROWS]
    back_ref[...] = acc[LOCAL_ROWS : LOCAL_ROWS + TILE].astype(BF16)


def layer(count, rows, cols, core, feat, halo, mine, other, adj, ws, wn, og):
    slots = adj.shape[0]
    hub_tiles, column_rows, _ = mine.shape
    sources = (ROW_BLOCKS + 1 + hub_tiles) * TILE
    parcel = jax.ShapeDtypeStruct((hub_tiles, column_rows + D // hub_tiles, D), BF16)
    smem = pl.BlockSpec(memory_space=pltpu.SMEM)
    vmem = pl.BlockSpec(memory_space=pltpu.VMEM)
    return pl.pallas_call(
        layer_kernel,
        out_shape=(
            jax.ShapeDtypeStruct((LOCAL_ROWS, D), BF16),
            jax.ShapeDtypeStruct((LOCAL_ROWS, D), F32),
            jax.ShapeDtypeStruct((TILE, D), BF16),
            parcel,
            parcel,
        ),
        in_specs=[smem] * 4 + [vmem] * 8,
        out_specs=(vmem,) * 5,
        scratch_shapes=[
            pltpu.VMEM((sources, D), BF16),
            pltpu.VMEM((LOCAL_ROWS, slots * TILE), BF16),
            pltpu.VMEM((slots * TILE, LOCAL_ROWS), BF16),
            pltpu.VMEM((slots * TILE, D), BF16),
            pltpu.VMEM((sources, D), F32),
        ],
        compiler_params=pltpu.CompilerParams(vmem_limit_bytes=48 * 1024 * 1024),
        name="layer",
    )(count, rows, cols, core, feat, halo, mine, other, adj, ws, wn, og)


def swap_cores(value):
    return lax.ppermute(value, "c", [(0, 1), (1, 0)])


def ring_shift(value, steps):
    count = 1
    for axis in ("y", "x", "z"):
        count *= lax.axis_size(axis)
    pairs = [(source, (source + steps) % count) for source in range(count)]
    return lax.ppermute(value, ("y", "x", "z"), pairs)


def exchange(value, axes):
    return lax.all_to_all(value, axes, 0, 0, tiled=True)


def spread(value, axes, count):
    return exchange(jnp.broadcast_to(value[None], (count,) + value.shape), axes)


def per_device(
    features,
    hub_feat,
    adjacency,
    block_row,
    block_col,
    block_count,
    halo_send,
    w_self,
    w_neigh,
    out_grad,
):
    zs = lax.axis_size("z")
    planes = lax.axis_size("y") * lax.axis_size("x")
    core = lax.axis_index("c").astype(jnp.int32)
    picks = halo_send[0]
    halo = ring_shift(features[picks], 1)
    column = spread(hub_feat, "z", zs).reshape(zs * OWN, D)
    mine = spread(column, PLANE, planes)
    other = swap_cores(mine)
    activations, base, back, keep, send = layer(
        block_count,
        block_row,
        block_col,
        core.reshape(1),
        features,
        halo,
        mine,
        other,
        adjacency,
        w_self,
        w_neigh,
        out_grad,
    )
    returned = ring_shift(back, -1)
    chip = (keep.astype(F32) + swap_cores(send).astype(F32)).astype(BF16)
    plane = jnp.sum(exchange(chip, PLANE).astype(F32), 0).astype(BF16)
    column_rows = zs * OWN
    hub_part = plane[:column_rows].reshape(zs, OWN, D)
    weight_part = plane[column_rows:]
    packed = jnp.concatenate(
        [hub_part, jnp.broadcast_to(weight_part[None], (zs,) + weight_part.shape)], 1
    )
    total = jnp.sum(exchange(packed, "z").astype(F32), 0)
    factor = 1.0 / math.sqrt(LOCAL_ROWS * 2 * zs * planes)
    weight_mine = spread((total[OWN:] * factor).astype(BF16), PLANE, planes).reshape(-1, D)
    weight_other = swap_cores(weight_mine)
    grad_w_self = jnp.where(core == 0, weight_mine, weight_other).astype(F32)
    grad_w_neigh = jnp.where(core == 0, weight_other, weight_mine).astype(F32)
    grad_features = base.at[picks].add(returned.astype(F32))
    return (activations, grad_features, total[:OWN], grad_w_self, grad_w_neigh)


def solution(mesh):
    inner = Mesh(mesh.devices.reshape(4, 4, 8, 2), ALL)
    in_specs = (
        P(ALL, None),
        P(ALL, None),
        P(ALL, None, None),
        P(ALL, None),
        P(ALL, None),
        P(ALL),
        P(ALL, None),
        P(),
        P(),
        P(ALL, None),
    )
    out_specs = (
        P(ALL, None),
        P(ALL, None),
        P(ALL, None),
        P(),
        P(),
    )
    return jax.shard_map(
        per_device, mesh=inner, in_specs=in_specs, out_specs=out_specs, check_vma=False
    )
```

```python
import math

import jax
import jax.numpy as jnp
from jax import lax
from jax.experimental import pallas as pl
from jax.experimental.pallas import tpu as pltpu
from jax.sharding import Mesh
from jax.sharding import PartitionSpec as P

D = 512
TILE = 128
ROW_BLOCKS = 2
LOCAL_ROWS = ROW_BLOCKS * TILE
OWN = 8
F32 = jnp.float32
BF16 = jnp.bfloat16
ALL = ("y", "x", "z", "c")
CHIPS = ("y", "x", "z")


def dot(a, b, contract=((1,), (0,))):
    return lax.dot_general(a, b, (contract, ((), ())), preferred_element_type=F32)


def prepare_kernel(
    count_ref, row_ref, adj_ref, feat_ref, ws_ref, wide_ref, flip_ref, norm_ref, pre_ref
):
    slots = adj_ref.shape[0]
    count = count_ref[0]
    degree = jnp.zeros((LOCAL_ROWS, TILE), F32)
    for s in range(slots):
        span = pl.ds(s * TILE, TILE)
        tile = adj_ref[s]
        flipped = tile.T
        blank = jnp.zeros_like(tile)
        parts = []
        for r in range(ROW_BLOCKS):
            on = (row_ref[0, s] == r) & (s < count)
            part = jnp.where(on, tile, blank)
            wide_ref[r * TILE : (r + 1) * TILE, span] = part
            flip_ref[span, r * TILE : (r + 1) * TILE] = jnp.where(on, flipped, blank)
            parts.append(part.astype(F32))
        degree += jnp.concatenate(parts, 0)
    norm = 1.0 / jnp.sqrt(1.0 + jnp.sum(degree, 1, keepdims=True))
    norm_ref[...] = jnp.broadcast_to(norm, (LOCAL_ROWS, TILE))
    pre_ref[...] = dot(feat_ref[...], ws_ref[...])


def layer_kernel(
    col_ref,
    core_ref,
    feat_ref,
    halo_ref,
    mine_ref,
    other_ref,
    wide_ref,
    flip_ref,
    norm_ref,
    pre_ref,
    ws_ref,
    wn_ref,
    og_ref,
    act_ref,
    base_ref,
    back_ref,
    keep_ref,
    send_ref,
    table,
    gathered,
    acc,
):
    slots = flip_ref.shape[0] // TILE
    hub_tiles, column_rows, _ = mine_ref.shape
    first_hub = ROW_BLOCKS + 1
    low_core = core_ref[0] == 0
    weight_rows = D // hub_tiles
    half = D * weight_rows // column_rows

    table[:LOCAL_ROWS] = feat_ref[...]
    table[LOCAL_ROWS : LOCAL_ROWS + TILE] = halo_ref[...]

    def fill(t, carry):
        here = mine_ref[t].astype(F32)
        there = other_ref[t].astype(F32)
        low = jnp.where(low_core, here, there)
        high = jnp.where(low_core, there, here)
        pieces = []
        for at in range(0, column_rows, OWN):
            pieces += [low[at : at + OWN], high[at : at + OWN]]
        start = pl.multiple_of((first_hub + t) * TILE, TILE)
        table[pl.ds(start, TILE)] = jnp.concatenate(pieces, 0).astype(BF16)
        return carry

    lax.fori_loop(0, hub_tiles, fill, 0)

    for s in range(slots):
        start = pl.multiple_of(col_ref[0, s] * TILE, TILE)
        gathered[s * TILE : (s + 1) * TILE] = table[pl.ds(start, TILE)]

    norm = jnp.concatenate([norm_ref[...]] * (D // TILE), 1)
    summed = dot(wide_ref[...], gathered[...])
    aggregate = (summed * norm).astype(BF16)
    own = feat_ref[...]
    preact = pre_ref[...] + dot(aggregate, wn_ref[...])
    gate = jax.nn.sigmoid(preact)
    act_ref[...] = (preact * gate).astype(BF16)
    grad_pre = (og_ref[...].astype(F32) * gate * (1.0 + preact * (1.0 - gate))).astype(BF16)
    grad_agg = (dot(grad_pre, wn_ref[...], ((1,), (1,))) * norm).astype(BF16)

    acc[...] = jnp.zeros_like(acc)
    for s in range(slots):
        into = pl.ds(pl.multiple_of(col_ref[0, s] * TILE, TILE), TILE)
        acc[into] += dot(flip_ref[s * TILE : (s + 1) * TILE], grad_agg)

    def ship(t, carry):
        start = pl.multiple_of((first_hub + t) * TILE, TILE)
        grads = acc[pl.ds(start, TILE)]
        low = jnp.concatenate([grads[at : at + OWN] for at in range(0, TILE, 2 * OWN)], 0)
        high = jnp.concatenate([grads[at + OWN : at + 2 * OWN] for at in range(0, TILE, 2 * OWN)], 0)
        keep_ref[t, :, :D] = jnp.where(low_core, low, high).astype(BF16)
        send_ref[t, :, :D] = jnp.where(low_core, high, low).astype(BF16)
        return carry

    lax.fori_loop(0, hub_tiles, ship, 0)

    grad_self_w = dot(own, grad_pre, ((0,), (0,)))
    grad_neigh_w = dot(aggregate, grad_pre, ((0,), (0,)))
    keep = jnp.where(low_core, grad_self_w, grad_neigh_w)
    send = jnp.where(low_core, grad_neigh_w, grad_self_w)
    for t in range(hub_tiles):
        for value, ref in ((keep, keep_ref), (send, send_ref)):
            pieces = []
            for z in range(column_rows // OWN):
                row = t * weight_rows + (z // 2) * OWN
                pieces.append(value[row : row + OWN, (z % 2) * half : (z % 2 + 1) * half])
            ref[t, :, D:] = jnp.concatenate(pieces, 0).astype(BF16)
    base_ref[...] = dot(grad_pre, ws_ref[...], ((1,), (1,))) + acc[:LOCAL_ROWS]
    back_ref[...] = acc[LOCAL_ROWS : LOCAL_ROWS + TILE].astype(BF16)


SMEM = pl.BlockSpec(memory_space=pltpu.SMEM)
VMEM = pl.BlockSpec(memory_space=pltpu.VMEM)


def prepare(count, rows, adj, feat, ws):
    wide = adj.shape[0] * TILE
    return pl.pallas_call(
        prepare_kernel,
        out_shape=(
            jax.ShapeDtypeStruct((LOCAL_ROWS, wide), BF16),
            jax.ShapeDtypeStruct((wide, LOCAL_ROWS), BF16),
            jax.ShapeDtypeStruct((LOCAL_ROWS, TILE), F32),
            jax.ShapeDtypeStruct((LOCAL_ROWS, D), F32),
        ),
        in_specs=[SMEM] * 2 + [VMEM] * 3,
        out_specs=(VMEM,) * 4,
        compiler_params=pltpu.CompilerParams(vmem_limit_bytes=16 * 1024 * 1024),
        cost_estimate=pl.CostEstimate(
            flops=2 * LOCAL_ROWS * D * D, bytes_accessed=5 * 1024 * 1024, transcendentals=0
        ),
        name="prepare",
    )(count, rows, adj, feat, ws)


def layer(cols, core, feat, halo, mine, other, wide, flip, norm, pre, ws, wn, og):
    hub_tiles, column_rows, _ = mine.shape
    sources = (ROW_BLOCKS + 1 + hub_tiles) * TILE
    parcel = jax.ShapeDtypeStruct((hub_tiles, column_rows, D + D * D // hub_tiles // column_rows), BF16)
    return pl.pallas_call(
        layer_kernel,
        out_shape=(
            jax.ShapeDtypeStruct((LOCAL_ROWS, D), BF16),
            jax.ShapeDtypeStruct((LOCAL_ROWS, D), F32),
            jax.ShapeDtypeStruct((TILE, D), BF16),
            parcel,
            parcel,
        ),
        in_specs=[SMEM] * 2 + [VMEM] * 11,
        out_specs=(VMEM,) * 5,
        scratch_shapes=[
            pltpu.VMEM((sources, D), BF16),
            pltpu.VMEM((wide.shape[1], D), BF16),
            pltpu.VMEM((sources, D), F32),
        ],
        compiler_params=pltpu.CompilerParams(vmem_limit_bytes=32 * 1024 * 1024),
        name="layer",
    )(cols, core, feat, halo, mine, other, wide, flip, norm, pre, ws, wn, og)


def swap_cores(value):
    return lax.ppermute(value, "c", [(0, 1), (1, 0)])


def ring_shift(value, steps):
    count = 1
    for axis in CHIPS:
        count *= lax.axis_size(axis)
    pairs = [(source, (source + steps) % count) for source in range(count)]
    return lax.ppermute(value, CHIPS, pairs)


def exchange(value):
    return lax.all_to_all(value, CHIPS, 0, 0, tiled=True)


def spread(value, count):
    return exchange(jnp.broadcast_to(value[None], (count,) + value.shape))


def per_device(
    features,
    hub_feat,
    adjacency,
    block_row,
    block_col,
    block_count,
    halo_send,
    w_self,
    w_neigh,
    out_grad,
):
    zs = lax.axis_size("z")
    planes = lax.axis_size("y") * lax.axis_size("x")
    chips = zs * planes
    core = lax.axis_index("c").astype(jnp.int32)
    picks = halo_send[0]
    chosen = (picks[:, None] == jnp.arange(LOCAL_ROWS, dtype=jnp.int32)[None, :]).astype(BF16)
    mine = spread(hub_feat, chips).reshape(planes, zs * OWN, D)
    halo = ring_shift(dot(chosen, features).astype(BF16), 1)
    wide, flip, norm, pre = prepare(block_count, block_row, adjacency, features, w_self)
    other = swap_cores(mine)
    activations, base, back, keep, send = layer(
        block_col,
        core.reshape(1),
        features,
        halo,
        mine,
        other,
        wide,
        flip,
        norm,
        pre,
        w_self,
        w_neigh,
        out_grad,
    )
    returned = ring_shift(back, -1)
    chip = (keep.astype(F32) + swap_cores(send).astype(F32)).astype(BF16)
    chip, returned = lax.optimization_barrier((chip, returned))
    total = jnp.sum(exchange(chip.reshape(chips, OWN, -1)).astype(F32), 0)
    factor = 1.0 / math.sqrt(LOCAL_ROWS * 2 * chips)
    weight_mine = spread((total[:, D:] * factor).astype(BF16), chips)
    weight_other = swap_cores(weight_mine)

    def unpack(value):
        rows = value.reshape(chips // 2, 2, OWN, -1)
        return jnp.transpose(rows, (0, 2, 1, 3)).reshape(D, D).astype(F32)

    grad_w_self = unpack(jnp.where(core == 0, weight_mine, weight_other))
    grad_w_neigh = unpack(jnp.where(core == 0, weight_other, weight_mine))
    grad_features = base + dot(chosen, returned, ((0,), (0,)))
    return (activations, grad_features, total[:, :D], grad_w_self, grad_w_neigh)


def solution(mesh):
    inner = Mesh(mesh.devices.reshape(4, 4, 8, 2), ALL)
    in_specs = (
        P(ALL, None),
        P(ALL, None),
        P(ALL, None, None),
        P(ALL, None),
        P(ALL, None),
        P(ALL),
        P(ALL, None),
        P(),
        P(),
        P(ALL, None),
    )
    out_specs = (
        P(ALL, None),
        P(ALL, None),
        P(ALL, None),
        P(),
        P(),
    )
    return jax.shard_map(
        per_device, mesh=inner, in_specs=in_specs, out_specs=out_specs, check_vma=False
    )
```

```python
import math

import jax
import jax.numpy as jnp
from jax import lax
from jax.experimental import pallas as pl
from jax.experimental.pallas import tpu as pltpu
from jax.sharding import Mesh
from jax.sharding import PartitionSpec as P

D = 512
TILE = 128
ROW_BLOCKS = 2
LOCAL_ROWS = ROW_BLOCKS * TILE
OWN = 8
F32 = jnp.float32
BF16 = jnp.bfloat16
ALL = ("y", "x", "z", "c")
CHIPS = ("y", "x", "z")
PLANE = ("y", "x")


def dot(a, b, contract=((1,), (0,))):
    return lax.dot_general(a, b, (contract, ((), ())), preferred_element_type=F32)


def prepare_kernel(
    count_ref, row_ref, adj_ref, feat_ref, ws_ref, wide_ref, flip_ref, norm_ref, pre_ref
):
    slots = adj_ref.shape[0]
    count = count_ref[0]
    degree = jnp.zeros((LOCAL_ROWS, TILE), F32)
    for s in range(slots):
        span = pl.ds(s * TILE, TILE)
        tile = adj_ref[s]
        flipped = tile.T
        blank = jnp.zeros_like(tile)
        parts = []
        for r in range(ROW_BLOCKS):
            on = (row_ref[0, s] == r) & (s < count)
            part = jnp.where(on, tile, blank)
            wide_ref[r * TILE : (r + 1) * TILE, span] = part
            flip_ref[span, r * TILE : (r + 1) * TILE] = jnp.where(on, flipped, blank)
            parts.append(part.astype(F32))
        degree += jnp.concatenate(parts, 0)
    norm = 1.0 / jnp.sqrt(1.0 + jnp.sum(degree, 1, keepdims=True))
    norm_ref[...] = jnp.broadcast_to(norm, (LOCAL_ROWS, TILE))
    pre_ref[...] = dot(feat_ref[...], ws_ref[...])


def layer_kernel(
    col_ref,
    core_ref,
    feat_ref,
    halo_ref,
    mine_ref,
    other_ref,
    wide_ref,
    flip_ref,
    norm_ref,
    pre_ref,
    ws_ref,
    wn_ref,
    og_ref,
    act_ref,
    base_ref,
    back_ref,
    keep_ref,
    send_ref,
    table,
    gathered,
    acc,
):
    slots = flip_ref.shape[0] // TILE
    hub_tiles, column_rows, _ = mine_ref.shape
    first_hub = ROW_BLOCKS + 1
    low_core = core_ref[0] == 0
    weight_rows = D // hub_tiles

    table[:LOCAL_ROWS] = feat_ref[...]
    table[LOCAL_ROWS : LOCAL_ROWS + TILE] = halo_ref[...]

    def fill(t, carry):
        here = mine_ref[t].astype(F32)
        there = other_ref[t].astype(F32)
        low = jnp.where(low_core, here, there)
        high = jnp.where(low_core, there, here)
        pieces = []
        for at in range(0, column_rows, OWN):
            pieces += [low[at : at + OWN], high[at : at + OWN]]
        start = pl.multiple_of((first_hub + t) * TILE, TILE)
        table[pl.ds(start, TILE)] = jnp.concatenate(pieces, 0).astype(BF16)
        return carry

    lax.fori_loop(0, hub_tiles, fill, 0)

    for s in range(slots):
        start = pl.multiple_of(col_ref[0, s] * TILE, TILE)
        gathered[s * TILE : (s + 1) * TILE] = table[pl.ds(start, TILE)]

    norm = jnp.concatenate([norm_ref[...]] * (D // TILE), 1)
    summed = dot(wide_ref[...], gathered[...])
    aggregate = (summed * norm).astype(BF16)
    own = feat_ref[...]
    preact = pre_ref[...] + dot(aggregate, wn_ref[...])
    gate = jax.nn.sigmoid(preact)
    act_ref[...] = (preact * gate).astype(BF16)
    grad_pre = (og_ref[...].astype(F32) * gate * (1.0 + preact * (1.0 - gate))).astype(BF16)
    grad_agg = (dot(grad_pre, wn_ref[...], ((1,), (1,))) * norm).astype(BF16)

    acc[...] = jnp.zeros_like(acc)
    for s in range(slots):
        into = pl.ds(pl.multiple_of(col_ref[0, s] * TILE, TILE), TILE)
        acc[into] += dot(flip_ref[s * TILE : (s + 1) * TILE], grad_agg)

    def ship(t, carry):
        start = pl.multiple_of((first_hub + t) * TILE, TILE)
        grads = acc[pl.ds(start, TILE)]
        low = jnp.concatenate([grads[at : at + OWN] for at in range(0, TILE, 2 * OWN)], 0)
        high = jnp.concatenate([grads[at + OWN : at + 2 * OWN] for at in range(0, TILE, 2 * OWN)], 0)
        keep_ref[t, :column_rows] = jnp.where(low_core, low, high).astype(BF16)
        send_ref[t, :column_rows] = jnp.where(low_core, high, low).astype(BF16)
        return carry

    lax.fori_loop(0, hub_tiles, ship, 0)

    grad_self_w = dot(own, grad_pre, ((0,), (0,)))
    grad_neigh_w = dot(aggregate, grad_pre, ((0,), (0,)))
    keep = jnp.where(low_core, grad_self_w, grad_neigh_w).astype(BF16)
    send = jnp.where(low_core, grad_neigh_w, grad_self_w).astype(BF16)
    keep_ref[:, column_rows:] = keep.reshape(hub_tiles, weight_rows, D)
    send_ref[:, column_rows:] = send.reshape(hub_tiles, weight_rows, D)
    base_ref[...] = dot(grad_pre, ws_ref[...], ((1,), (1,))) + acc[:LOCAL_ROWS]
    back_ref[...] = acc[LOCAL_ROWS : LOCAL_ROWS + TILE].astype(BF16)


SMEM = pl.BlockSpec(memory_space=pltpu.SMEM)
VMEM = pl.BlockSpec(memory_space=pltpu.VMEM)


def prepare(count, rows, adj, feat, ws):
    wide = adj.shape[0] * TILE
    return pl.pallas_call(
        prepare_kernel,
        out_shape=(
            jax.ShapeDtypeStruct((LOCAL_ROWS, wide), BF16),
            jax.ShapeDtypeStruct((wide, LOCAL_ROWS), BF16),
            jax.ShapeDtypeStruct((LOCAL_ROWS, TILE), F32),
            jax.ShapeDtypeStruct((LOCAL_ROWS, D), F32),
        ),
        in_specs=[SMEM] * 2 + [VMEM] * 3,
        out_specs=(VMEM,) * 4,
        compiler_params=pltpu.CompilerParams(vmem_limit_bytes=16 * 1024 * 1024),
        cost_estimate=pl.CostEstimate(
            flops=2 * LOCAL_ROWS * D * D, bytes_accessed=5 * 1024 * 1024, transcendentals=0
        ),
        name="prepare",
    )(count, rows, adj, feat, ws)


def layer(cols, core, feat, halo, mine, other, wide, flip, norm, pre, ws, wn, og):
    hub_tiles, column_rows, _ = mine.shape
    sources = (ROW_BLOCKS + 1 + hub_tiles) * TILE
    parcel = jax.ShapeDtypeStruct((hub_tiles, column_rows + D // hub_tiles, D), BF16)
    return pl.pallas_call(
        layer_kernel,
        out_shape=(
            jax.ShapeDtypeStruct((LOCAL_ROWS, D), BF16),
            jax.ShapeDtypeStruct((LOCAL_ROWS, D), F32),
            jax.ShapeDtypeStruct((TILE, D), BF16),
            parcel,
            parcel,
        ),
        in_specs=[SMEM] * 2 + [VMEM] * 11,
        out_specs=(VMEM,) * 5,
        scratch_shapes=[
            pltpu.VMEM((sources, D), BF16),
            pltpu.VMEM((wide.shape[1], D), BF16),
            pltpu.VMEM((sources, D), F32),
        ],
        compiler_params=pltpu.CompilerParams(vmem_limit_bytes=32 * 1024 * 1024),
        name="layer",
    )(cols, core, feat, halo, mine, other, wide, flip, norm, pre, ws, wn, og)


def swap_cores(value):
    return lax.ppermute(value, "c", [(0, 1), (1, 0)])


def ring_shift(value, steps):
    count = 1
    for axis in CHIPS:
        count *= lax.axis_size(axis)
    pairs = [(source, (source + steps) % count) for source in range(count)]
    return lax.ppermute(value, CHIPS, pairs)


def exchange(value, axes):
    return lax.all_to_all(value, axes, 0, 0, tiled=True)


def spread(value, axes):
    count = math.prod(lax.axis_size(axis) for axis in axes)
    return exchange(jnp.broadcast_to(value[None], (count,) + value.shape), axes)


def per_device(
    features,
    hub_feat,
    adjacency,
    block_row,
    block_col,
    block_count,
    halo_send,
    w_self,
    w_neigh,
    out_grad,
):
    zs = lax.axis_size("z")
    planes = lax.axis_size("y") * lax.axis_size("x")
    chips = zs * planes
    core = lax.axis_index("c").astype(jnp.int32)
    picks = halo_send[0]
    chosen = (picks[:, None] == jnp.arange(LOCAL_ROWS, dtype=jnp.int32)[None, :]).astype(BF16)
    halo = ring_shift(dot(chosen, features).astype(BF16), 1)
    column = spread(hub_feat, ("z",)).reshape(zs * OWN, D)
    column, halo = lax.optimization_barrier((column, halo))
    mine = spread(column, PLANE)
    wide, flip, norm, pre = prepare(block_count, block_row, adjacency, features, w_self)
    other = swap_cores(mine)
    activations, base, back, keep, send = layer(
        block_col,
        core.reshape(1),
        features,
        halo,
        mine,
        other,
        wide,
        flip,
        norm,
        pre,
        w_self,
        w_neigh,
        out_grad,
    )
    returned = ring_shift(back, -1)
    chip = (keep.astype(F32) + swap_cores(send).astype(F32)).astype(BF16)
    plane = jnp.sum(exchange(chip, PLANE).astype(F32), 0).astype(BF16)
    plane, returned = lax.optimization_barrier((plane, returned))
    column_rows = zs * OWN
    hub_part = plane[:column_rows].reshape(zs, OWN, D)
    weight_part = plane[column_rows:]
    packed = jnp.concatenate(
        [hub_part, jnp.broadcast_to(weight_part[None], (zs,) + weight_part.shape)], 1
    )
    total = jnp.sum(exchange(packed, ("z",)).astype(F32), 0)
    factor = 1.0 / math.sqrt(LOCAL_ROWS * 2 * chips)
    weight_mine = spread((total[OWN:] * factor).astype(BF16), PLANE).reshape(D, D)
    weight_other = swap_cores(weight_mine)
    grad_w_self = jnp.where(core == 0, weight_mine, weight_other).astype(F32)
    grad_w_neigh = jnp.where(core == 0, weight_other, weight_mine).astype(F32)
    grad_features = base + dot(chosen, returned, ((0,), (0,)))
    return (activations, grad_features, total[:OWN], grad_w_self, grad_w_neigh)


def solution(mesh):
    inner = Mesh(mesh.devices.reshape(4, 4, 8, 2), ALL)
    in_specs = (
        P(ALL, None),
        P(ALL, None),
        P(ALL, None, None),
        P(ALL, None),
        P(ALL, None),
        P(ALL),
        P(ALL, None),
        P(),
        P(),
        P(ALL, None),
    )
    out_specs = (
        P(ALL, None),
        P(ALL, None),
        P(ALL, None),
        P(),
        P(),
    )
    return jax.shard_map(
        per_device, mesh=inner, in_specs=in_specs, out_specs=out_specs, check_vma=False
    )
```

```python
import math

import jax
import jax.numpy as jnp
from jax import lax
from jax.experimental import pallas as pl
from jax.experimental.pallas import tpu as pltpu
from jax.sharding import Mesh
from jax.sharding import PartitionSpec as P

D = 512
TILE = 128
ROW_BLOCKS = 2
LOCAL_ROWS = ROW_BLOCKS * TILE
OWN = 8
F32 = jnp.float32
BF16 = jnp.bfloat16
ALL = ("y", "x", "z", "c")
CHIPS = ("y", "x", "z")
PLANE = ("y", "x")


def dot(a, b, contract=((1,), (0,))):
    return lax.dot_general(a, b, (contract, ((), ())), preferred_element_type=F32)


def prepare_kernel(
    count_ref, row_ref, adj_ref, feat_ref, ws_ref, wide_ref, flip_ref, norm_ref, pre_ref
):
    slots = adj_ref.shape[0]
    count = count_ref[0]
    degree = jnp.zeros((LOCAL_ROWS, TILE), F32)
    for s in range(slots):
        span = pl.ds(s * TILE, TILE)
        tile = adj_ref[s]
        flipped = tile.T
        blank = jnp.zeros_like(tile)
        parts = []
        for r in range(ROW_BLOCKS):
            on = (row_ref[0, s] == r) & (s < count)
            part = jnp.where(on, tile, blank)
            wide_ref[r * TILE : (r + 1) * TILE, span] = part
            flip_ref[span, r * TILE : (r + 1) * TILE] = jnp.where(on, flipped, blank)
            parts.append(part.astype(F32))
        degree += jnp.concatenate(parts, 0)
    norm = 1.0 / jnp.sqrt(1.0 + jnp.sum(degree, 1, keepdims=True))
    norm_ref[...] = jnp.broadcast_to(norm, (LOCAL_ROWS, TILE))
    pre_ref[...] = dot(feat_ref[...], ws_ref[...])


def forward_kernel(
    col_ref,
    core_ref,
    feat_ref,
    halo_ref,
    mine_ref,
    other_ref,
    wide_ref,
    flip_ref,
    norm_ref,
    pre_ref,
    wn_ref,
    og_ref,
    act_ref,
    agg_ref,
    grad_pre_ref,
    grad_agg_ref,
    back_ref,
    table,
    gathered,
    acc,
):
    slots = flip_ref.shape[0] // TILE
    hub_tiles, column_rows, _ = mine_ref.shape
    first_hub = ROW_BLOCKS + 1
    low_core = core_ref[0] == 0

    table[:LOCAL_ROWS] = feat_ref[...]
    table[LOCAL_ROWS : LOCAL_ROWS + TILE] = halo_ref[...]

    def fill(t, carry):
        here = mine_ref[t].astype(F32)
        there = other_ref[t].astype(F32)
        low = jnp.where(low_core, here, there)
        high = jnp.where(low_core, there, here)
        pieces = []
        for at in range(0, column_rows, OWN):
            pieces += [low[at : at + OWN], high[at : at + OWN]]
        start = pl.multiple_of((first_hub + t) * TILE, TILE)
        table[pl.ds(start, TILE)] = jnp.concatenate(pieces, 0).astype(BF16)
        return carry

    lax.fori_loop(0, hub_tiles, fill, 0)

    for s in range(slots):
        start = pl.multiple_of(col_ref[0, s] * TILE, TILE)
        gathered[s * TILE : (s + 1) * TILE] = table[pl.ds(start, TILE)]

    norm = jnp.concatenate([norm_ref[...]] * (D // TILE), 1)
    summed = dot(wide_ref[...], gathered[...])
    aggregate = (summed * norm).astype(BF16)
    agg_ref[...] = aggregate
    preact = pre_ref[...] + dot(aggregate, wn_ref[...])
    gate = jax.nn.sigmoid(preact)
    act_ref[...] = (preact * gate).astype(BF16)
    grad_pre = (og_ref[...].astype(F32) * gate * (1.0 + preact * (1.0 - gate))).astype(BF16)
    grad_pre_ref[...] = grad_pre
    grad_agg = (dot(grad_pre, wn_ref[...], ((1,), (1,))) * norm).astype(BF16)
    grad_agg_ref[...] = grad_agg

    acc[...] = jnp.zeros_like(acc)
    for s in range(slots):

        @pl.when(col_ref[0, s] == ROW_BLOCKS)
        def _(s=s):
            acc[...] += dot(flip_ref[s * TILE : (s + 1) * TILE], grad_agg_ref[...])

    back_ref[...] = acc[...].astype(BF16)


def backward_kernel(
    col_ref,
    core_ref,
    feat_ref,
    flip_ref,
    agg_ref,
    grad_pre_ref,
    grad_agg_ref,
    ws_ref,
    base_ref,
    keep_ref,
    send_ref,
    acc,
):
    slots = flip_ref.shape[0] // TILE
    hub_tiles, parcel_rows, _ = keep_ref.shape
    weight_rows = D // hub_tiles
    column_rows = parcel_rows - weight_rows
    first_hub = ROW_BLOCKS + 1
    low_core = core_ref[0] == 0

    acc[...] = jnp.zeros_like(acc)
    for s in range(slots):
        into = pl.ds(pl.multiple_of(col_ref[0, s] * TILE, TILE), TILE)
        acc[into] += dot(flip_ref[s * TILE : (s + 1) * TILE], grad_agg_ref[...])

    def ship(t, carry):
        start = pl.multiple_of((first_hub + t) * TILE, TILE)
        grads = acc[pl.ds(start, TILE)]
        low = jnp.concatenate([grads[at : at + OWN] for at in range(0, TILE, 2 * OWN)], 0)
        high = jnp.concatenate([grads[at + OWN : at + 2 * OWN] for at in range(0, TILE, 2 * OWN)], 0)
        keep_ref[t, :column_rows] = jnp.where(low_core, low, high).astype(BF16)
        send_ref[t, :column_rows] = jnp.where(low_core, high, low).astype(BF16)
        return carry

    lax.fori_loop(0, hub_tiles, ship, 0)

    grad_pre = grad_pre_ref[...]
    grad_self_w = dot(feat_ref[...], grad_pre, ((0,), (0,)))
    grad_neigh_w = dot(agg_ref[...], grad_pre, ((0,), (0,)))
    keep = jnp.where(low_core, grad_self_w, grad_neigh_w).astype(BF16)
    send = jnp.where(low_core, grad_neigh_w, grad_self_w).astype(BF16)
    keep_ref[:, column_rows:] = keep.reshape(hub_tiles, weight_rows, D)
    send_ref[:, column_rows:] = send.reshape(hub_tiles, weight_rows, D)
    base_ref[...] = dot(grad_pre, ws_ref[...], ((1,), (1,))) + acc[:LOCAL_ROWS]


SMEM = pl.BlockSpec(memory_space=pltpu.SMEM)
VMEM = pl.BlockSpec(memory_space=pltpu.VMEM)


def prepare(count, rows, adj, feat, ws):
    wide = adj.shape[0] * TILE
    return pl.pallas_call(
        prepare_kernel,
        out_shape=(
            jax.ShapeDtypeStruct((LOCAL_ROWS, wide), BF16),
            jax.ShapeDtypeStruct((wide, LOCAL_ROWS), BF16),
            jax.ShapeDtypeStruct((LOCAL_ROWS, TILE), F32),
            jax.ShapeDtypeStruct((LOCAL_ROWS, D), F32),
        ),
        in_specs=[SMEM] * 2 + [VMEM] * 3,
        out_specs=(VMEM,) * 4,
        compiler_params=pltpu.CompilerParams(vmem_limit_bytes=16 * 1024 * 1024),
        cost_estimate=pl.CostEstimate(
            flops=2 * LOCAL_ROWS * D * D, bytes_accessed=5 * 1024 * 1024, transcendentals=0
        ),
        name="prepare",
    )(count, rows, adj, feat, ws)


def forward(cols, core, feat, halo, mine, other, wide, flip, norm, pre, wn, og):
    hub_tiles = mine.shape[0]
    sources = (ROW_BLOCKS + 1 + hub_tiles) * TILE
    local = jax.ShapeDtypeStruct((LOCAL_ROWS, D), BF16)
    return pl.pallas_call(
        forward_kernel,
        out_shape=(local, local, local, local, jax.ShapeDtypeStruct((TILE, D), BF16)),
        in_specs=[SMEM] * 2 + [VMEM] * 10,
        out_specs=(VMEM,) * 5,
        scratch_shapes=[
            pltpu.VMEM((sources, D), BF16),
            pltpu.VMEM((wide.shape[1], D), BF16),
            pltpu.VMEM((TILE, D), F32),
        ],
        compiler_params=pltpu.CompilerParams(vmem_limit_bytes=16 * 1024 * 1024),
        name="forward",
    )(cols, core, feat, halo, mine, other, wide, flip, norm, pre, wn, og)


def backward(cols, core, feat, flip, agg, grad_pre, grad_agg, ws, hub_tiles, column_rows):
    sources = (ROW_BLOCKS + 1 + hub_tiles) * TILE
    parcel = jax.ShapeDtypeStruct((hub_tiles, column_rows + D // hub_tiles, D), BF16)
    return pl.pallas_call(
        backward_kernel,
        out_shape=(jax.ShapeDtypeStruct((LOCAL_ROWS, D), F32), parcel, parcel),
        in_specs=[SMEM] * 2 + [VMEM] * 6,
        out_specs=(VMEM,) * 3,
        scratch_shapes=[pltpu.VMEM((sources, D), F32)],
        compiler_params=pltpu.CompilerParams(vmem_limit_bytes=16 * 1024 * 1024),
        name="backward",
    )(cols, core, feat, flip, agg, grad_pre, grad_agg, ws)


def swap_cores(value):
    return lax.ppermute(value, "c", [(0, 1), (1, 0)])


def ring_shift(value, steps):
    count = 1
    for axis in CHIPS:
        count *= lax.axis_size(axis)
    pairs = [(source, (source + steps) % count) for source in range(count)]
    return lax.ppermute(value, CHIPS, pairs)


def exchange(value, axes):
    return lax.all_to_all(value, axes, 0, 0, tiled=True)


def spread(value, axes):
    count = math.prod(lax.axis_size(axis) for axis in axes)
    return exchange(jnp.broadcast_to(value[None], (count,) + value.shape), axes)


def per_device(
    features,
    hub_feat,
    adjacency,
    block_row,
    block_col,
    block_count,
    halo_send,
    w_self,
    w_neigh,
    out_grad,
):
    zs = lax.axis_size("z")
    planes = lax.axis_size("y") * lax.axis_size("x")
    chips = zs * planes
    core = lax.axis_index("c").astype(jnp.int32)
    picks = halo_send[0]
    chosen = (picks[:, None] == jnp.arange(LOCAL_ROWS, dtype=jnp.int32)[None, :]).astype(BF16)
    halo = ring_shift(dot(chosen, features).astype(BF16), 1)
    column = spread(hub_feat, ("z",)).reshape(zs * OWN, D)
    column, halo = lax.optimization_barrier((column, halo))
    mine = spread(column, PLANE)
    wide, flip, norm, pre = prepare(block_count, block_row, adjacency, features, w_self)
    other = swap_cores(mine)
    scalar = core.reshape(1)
    activations, aggregate, grad_pre, grad_agg, back = forward(
        block_col,
        scalar,
        features,
        halo,
        mine,
        other,
        wide,
        flip,
        norm,
        pre,
        w_neigh,
        out_grad,
    )
    returned = ring_shift(back, -1)
    base, keep, send = backward(
        block_col,
        scalar,
        features,
        flip,
        aggregate,
        grad_pre,
        grad_agg,
        w_self,
        planes,
        zs * OWN,
    )
    chip = (keep.astype(F32) + swap_cores(send).astype(F32)).astype(BF16)
    plane = jnp.sum(exchange(chip, PLANE).astype(F32), 0).astype(BF16)
    column_rows = zs * OWN
    hub_part = plane[:column_rows].reshape(zs, OWN, D)
    weight_part = plane[column_rows:]
    packed = jnp.concatenate(
        [hub_part, jnp.broadcast_to(weight_part[None], (zs,) + weight_part.shape)], 1
    )
    total = jnp.sum(exchange(packed, ("z",)).astype(F32), 0)
    factor = 1.0 / math.sqrt(LOCAL_ROWS * 2 * chips)
    weight_mine = spread((total[OWN:] * factor).astype(BF16), PLANE).reshape(D, D)
    weight_mine, returned = lax.optimization_barrier((weight_mine, returned))
    weight_other = swap_cores(weight_mine)
    grad_w_self = jnp.where(core == 0, weight_mine, weight_other).astype(F32)
    grad_w_neigh = jnp.where(core == 0, weight_other, weight_mine).astype(F32)
    grad_features = base + dot(chosen, returned, ((0,), (0,)))
    return (activations, grad_features, total[:OWN], grad_w_self, grad_w_neigh)


def solution(mesh):
    inner = Mesh(mesh.devices.reshape(4, 4, 8, 2), ALL)
    in_specs = (
        P(ALL, None),
        P(ALL, None),
        P(ALL, None, None),
        P(ALL, None),
        P(ALL, None),
        P(ALL),
        P(ALL, None),
        P(),
        P(),
        P(ALL, None),
    )
    out_specs = (
        P(ALL, None),
        P(ALL, None),
        P(ALL, None),
        P(),
        P(),
    )
    return jax.shard_map(
        per_device, mesh=inner, in_specs=in_specs, out_specs=out_specs, check_vma=False
    )
```

```python
import math

import jax
import jax.numpy as jnp
from jax import lax
from jax.experimental import pallas as pl
from jax.experimental.pallas import tpu as pltpu
from jax.sharding import Mesh
from jax.sharding import PartitionSpec as P

D = 512
TILE = 128
ROW_BLOCKS = 2
LOCAL_ROWS = ROW_BLOCKS * TILE
OWN = 8
F32 = jnp.float32
BF16 = jnp.bfloat16
ALL = ("y", "x", "z", "c")
CHIPS = ("y", "x", "z")
PLANE = ("y", "x")
SIDE = 4
ZS = 8


def dot(a, b, contract=((1,), (0,))):
    return lax.dot_general(a, b, (contract, ((), ())), preferred_element_type=F32)


def prepare_kernel(
    count_ref, row_ref, adj_ref, feat_ref, ws_ref, wide_ref, flip_ref, norm_ref, pre_ref
):
    slots = adj_ref.shape[0]
    count = count_ref[0]
    degree = jnp.zeros((LOCAL_ROWS, TILE), F32)
    for s in range(slots):
        span = pl.ds(s * TILE, TILE)
        tile = adj_ref[s]
        flipped = tile.T
        blank = jnp.zeros_like(tile)
        parts = []
        for r in range(ROW_BLOCKS):
            on = (row_ref[0, s] == r) & (s < count)
            part = jnp.where(on, tile, blank)
            wide_ref[r * TILE : (r + 1) * TILE, span] = part
            flip_ref[span, r * TILE : (r + 1) * TILE] = jnp.where(on, flipped, blank)
            parts.append(part.astype(F32))
        degree += jnp.concatenate(parts, 0)
    norm = 1.0 / jnp.sqrt(1.0 + jnp.sum(degree, 1, keepdims=True))
    norm_ref[...] = jnp.broadcast_to(norm, (LOCAL_ROWS, TILE))
    pre_ref[...] = dot(feat_ref[...], ws_ref[...])


def layer_kernel(
    col_ref,
    spot_ref,
    feat_ref,
    halo_ref,
    mine_ref,
    other_ref,
    wide_ref,
    flip_ref,
    norm_ref,
    pre_ref,
    ws_ref,
    wn_ref,
    og_ref,
    act_ref,
    base_ref,
    back_ref,
    keep_ref,
    send_ref,
    table,
    gathered,
    acc,
):
    slots = flip_ref.shape[0] // TILE
    hub_tiles, column_rows, _ = mine_ref.shape
    first_hub = ROW_BLOCKS + 1
    low_core = spot_ref[0] == 0
    y, x = spot_ref[1], spot_ref[2]

    def order(tile, sign):
        down = (tile // SIDE - y) * sign & (SIDE - 1)
        along = (tile % SIDE - x) * sign & (SIDE - 1)
        down_first, along_first = down * SIDE + along, along * SIDE + down
        mine = jnp.where(low_core, down_first, along_first)
        return mine, jnp.where(low_core, along_first, down_first)

    weight_rows = D // hub_tiles

    table[:LOCAL_ROWS] = feat_ref[...]
    table[LOCAL_ROWS : LOCAL_ROWS + TILE] = halo_ref[...]

    def fill(t, carry):
        here_at, there_at = order(t, -1)
        here = mine_ref[here_at].astype(F32)
        there = other_ref[there_at].astype(F32)
        low = jnp.where(low_core, here, there)
        high = jnp.where(low_core, there, here)
        pieces = []
        for at in range(0, column_rows, OWN):
            pieces += [low[at : at + OWN], high[at : at + OWN]]
        start = pl.multiple_of((first_hub + t) * TILE, TILE)
        table[pl.ds(start, TILE)] = jnp.concatenate(pieces, 0).astype(BF16)
        return carry

    lax.fori_loop(0, hub_tiles, fill, 0)

    for s in range(slots):
        start = pl.multiple_of(col_ref[0, s] * TILE, TILE)
        gathered[s * TILE : (s + 1) * TILE] = table[pl.ds(start, TILE)]

    norm = jnp.concatenate([norm_ref[...]] * (D // TILE), 1)
    summed = dot(wide_ref[...], gathered[...])
    aggregate = (summed * norm).astype(BF16)
    own = feat_ref[...]
    preact = pre_ref[...] + dot(aggregate, wn_ref[...])
    gate = jax.nn.sigmoid(preact)
    act_ref[...] = (preact * gate).astype(BF16)
    grad_pre = (og_ref[...].astype(F32) * gate * (1.0 + preact * (1.0 - gate))).astype(BF16)
    grad_agg = (dot(grad_pre, wn_ref[...], ((1,), (1,))) * norm).astype(BF16)

    acc[...] = jnp.zeros_like(acc)
    for s in range(slots):
        into = pl.ds(pl.multiple_of(col_ref[0, s] * TILE, TILE), TILE)
        acc[into] += dot(flip_ref[s * TILE : (s + 1) * TILE], grad_agg)

    def ship(t, carry):
        start = pl.multiple_of((first_hub + t) * TILE, TILE)
        grads = acc[pl.ds(start, TILE)]
        low = jnp.concatenate([grads[at : at + OWN] for at in range(0, TILE, 2 * OWN)], 0)
        high = jnp.concatenate([grads[at + OWN : at + 2 * OWN] for at in range(0, TILE, 2 * OWN)], 0)
        keep_at, send_at = order(t, 1)
        keep_ref[keep_at, :column_rows] = jnp.where(low_core, low, high).astype(BF16)
        send_ref[send_at, :column_rows] = jnp.where(low_core, high, low).astype(BF16)
        return carry

    lax.fori_loop(0, hub_tiles, ship, 0)

    grad_self_w = dot(own, grad_pre, ((0,), (0,)))
    grad_neigh_w = dot(aggregate, grad_pre, ((0,), (0,)))
    keep = jnp.where(low_core, grad_self_w, grad_neigh_w).astype(BF16)
    send = jnp.where(low_core, grad_neigh_w, grad_self_w).astype(BF16)
    for t in range(hub_tiles):
        keep_at, send_at = order(t, 1)
        keep_ref[keep_at, column_rows:] = keep[t * weight_rows : (t + 1) * weight_rows]
        send_ref[send_at, column_rows:] = send[t * weight_rows : (t + 1) * weight_rows]
    base_ref[...] = dot(grad_pre, ws_ref[...], ((1,), (1,))) + acc[:LOCAL_ROWS]
    back_ref[...] = acc[LOCAL_ROWS : LOCAL_ROWS + TILE].astype(BF16)


SMEM = pl.BlockSpec(memory_space=pltpu.SMEM)
VMEM = pl.BlockSpec(memory_space=pltpu.VMEM)


def prepare(count, rows, adj, feat, ws):
    wide = adj.shape[0] * TILE
    return pl.pallas_call(
        prepare_kernel,
        out_shape=(
            jax.ShapeDtypeStruct((LOCAL_ROWS, wide), BF16),
            jax.ShapeDtypeStruct((wide, LOCAL_ROWS), BF16),
            jax.ShapeDtypeStruct((LOCAL_ROWS, TILE), F32),
            jax.ShapeDtypeStruct((LOCAL_ROWS, D), F32),
        ),
        in_specs=[SMEM] * 2 + [VMEM] * 3,
        out_specs=(VMEM,) * 4,
        compiler_params=pltpu.CompilerParams(vmem_limit_bytes=16 * 1024 * 1024),
        cost_estimate=pl.CostEstimate(
            flops=2 * LOCAL_ROWS * D * D, bytes_accessed=5 * 1024 * 1024, transcendentals=0
        ),
        name="prepare",
    )(count, rows, adj, feat, ws)


def layer(cols, core, feat, halo, mine, other, wide, flip, norm, pre, ws, wn, og):
    hub_tiles, column_rows, _ = mine.shape
    sources = (ROW_BLOCKS + 1 + hub_tiles) * TILE
    parcel = jax.ShapeDtypeStruct((hub_tiles, column_rows + D // hub_tiles, D), BF16)
    return pl.pallas_call(
        layer_kernel,
        out_shape=(
            jax.ShapeDtypeStruct((LOCAL_ROWS, D), BF16),
            jax.ShapeDtypeStruct((LOCAL_ROWS, D), F32),
            jax.ShapeDtypeStruct((TILE, D), BF16),
            parcel,
            parcel,
        ),
        in_specs=[SMEM] * 2 + [VMEM] * 11,
        out_specs=(VMEM,) * 5,
        scratch_shapes=[
            pltpu.VMEM((sources, D), BF16),
            pltpu.VMEM((wide.shape[1], D), BF16),
            pltpu.VMEM((sources, D), F32),
        ],
        compiler_params=pltpu.CompilerParams(vmem_limit_bytes=16 * 1024 * 1024),
        name="layer",
    )(cols, core, feat, halo, mine, other, wide, flip, norm, pre, ws, wn, og)


def swap_cores(value):
    return lax.ppermute(value, "c", [(0, 1), (1, 0)])


def ring_shift(value, steps):
    count = 1
    for axis in CHIPS:
        count *= lax.axis_size(axis)
    pairs = [(source, (source + steps) % count) for source in range(count)]
    return lax.ppermute(value, CHIPS, pairs)


def place(y, x, z, c):
    return ((y % SIDE * SIDE + x % SIDE) * ZS + z) * 2 + c


def hop(value, first, steps):
    pairs = []
    for y in range(SIDE):
        for x in range(SIDE):
            for c in (0, 1):
                down = steps if (c == 0) == first else 0
                for z in range(ZS):
                    pairs.append((place(y, x, z, c), place(y + down, x + steps - down, z, c)))
    return lax.ppermute(value, ALL, pairs)


def add_along(parts, first):
    came = [hop(parts[k], first, k) for k in (2, 1, 3)]
    total = parts[0].astype(F32)
    for part in came:
        total += part.astype(F32)
    return total.astype(BF16)


def collect(value, first):
    far, near, back = (hop(value, first, k) for k in (2, 1, 3))
    return jnp.concatenate([value, near, far, back], 0)


def exchange(value, axes):
    return lax.all_to_all(value, axes, 0, 0, tiled=True)


def spread(value, axes):
    count = math.prod(lax.axis_size(axis) for axis in axes)
    return exchange(jnp.broadcast_to(value[None], (count,) + value.shape), axes)


def per_device(
    features,
    hub_feat,
    adjacency,
    block_row,
    block_col,
    block_count,
    halo_send,
    w_self,
    w_neigh,
    out_grad,
):
    zs = lax.axis_size("z")
    planes = lax.axis_size("y") * lax.axis_size("x")
    chips = zs * planes
    core = lax.axis_index("c").astype(jnp.int32)
    picks = halo_send[0]
    chosen = (picks[:, None] == jnp.arange(LOCAL_ROWS, dtype=jnp.int32)[None, :]).astype(BF16)
    halo = ring_shift(dot(chosen, features).astype(BF16), 1)
    column = spread(hub_feat, ("z",)).reshape(zs * OWN, D)
    mine = collect(collect(column, False), True).reshape(planes, zs * OWN, D)
    mine, halo = lax.optimization_barrier((mine, halo))
    wide, flip, norm, pre = prepare(block_count, block_row, adjacency, features, w_self)
    other = swap_cores(mine)
    activations, base, back, keep, send = layer(
        block_col,
        jnp.stack([core, lax.axis_index("y"), lax.axis_index("x")]).astype(jnp.int32),
        features,
        halo,
        mine,
        other,
        wide,
        flip,
        norm,
        pre,
        w_self,
        w_neigh,
        out_grad,
    )
    returned = ring_shift(back, -1)
    chip = (keep.astype(F32) + swap_cores(send).astype(F32)).astype(BF16)
    lines = add_along(chip.reshape(SIDE, SIDE, -1, D), True)
    plane = add_along(lines, False)
    column_rows = zs * OWN
    hub_part = plane[:column_rows].reshape(zs, OWN, D)
    weight_part = plane[column_rows:]
    packed = jnp.concatenate(
        [hub_part, jnp.broadcast_to(weight_part[None], (zs,) + weight_part.shape)], 1
    )
    total = jnp.sum(exchange(packed, ("z",)).astype(F32), 0)
    factor = 1.0 / math.sqrt(LOCAL_ROWS * 2 * chips)
    weight_mine = spread((total[OWN:] * factor).astype(BF16), PLANE).reshape(D, D)
    weight_mine, returned = lax.optimization_barrier((weight_mine, returned))
    weight_other = swap_cores(weight_mine)
    grad_w_self = jnp.where(core == 0, weight_mine, weight_other).astype(F32)
    grad_w_neigh = jnp.where(core == 0, weight_other, weight_mine).astype(F32)
    grad_features = base + dot(chosen, returned, ((0,), (0,)))
    return (activations, grad_features, total[:OWN], grad_w_self, grad_w_neigh)


def solution(mesh):
    inner = Mesh(mesh.devices.reshape(4, 4, 8, 2), ALL)
    in_specs = (
        P(ALL, None),
        P(ALL, None),
        P(ALL, None, None),
        P(ALL, None),
        P(ALL, None),
        P(ALL),
        P(ALL, None),
        P(),
        P(),
        P(ALL, None),
    )
    out_specs = (
        P(ALL, None),
        P(ALL, None),
        P(ALL, None),
        P(),
        P(),
    )
    return jax.shard_map(
        per_device, mesh=inner, in_specs=in_specs, out_specs=out_specs, check_vma=False
    )
```

```python
import math

import jax
import jax.numpy as jnp
from jax import lax
from jax.experimental import pallas as pl
from jax.experimental.pallas import tpu as pltpu
from jax.sharding import Mesh
from jax.sharding import PartitionSpec as P

D = 512
TILE = 128
ROW_BLOCKS = 2
LOCAL_ROWS = ROW_BLOCKS * TILE
OWN = 8
F32 = jnp.float32
BF16 = jnp.bfloat16
ALL = ("y", "x", "z", "c")
CHIPS = ("y", "x", "z")
PLANE = ("y", "x")
SIDE = 4
ZS = 8


def dot(a, b, contract=((1,), (0,))):
    return lax.dot_general(a, b, (contract, ((), ())), preferred_element_type=F32)


def prepare_kernel(
    count_ref, row_ref, adj_ref, feat_ref, ws_ref, wide_ref, flip_ref, norm_ref, pre_ref
):
    slots = adj_ref.shape[0]
    count = count_ref[0]
    degree = jnp.zeros((LOCAL_ROWS, TILE), F32)
    for s in range(slots):
        span = pl.ds(s * TILE, TILE)
        tile = adj_ref[s]
        flipped = tile.T
        blank = jnp.zeros_like(tile)
        parts = []
        for r in range(ROW_BLOCKS):
            on = (row_ref[0, s] == r) & (s < count)
            part = jnp.where(on, tile, blank)
            wide_ref[r * TILE : (r + 1) * TILE, span] = part
            flip_ref[span, r * TILE : (r + 1) * TILE] = jnp.where(on, flipped, blank)
            parts.append(part.astype(F32))
        degree += jnp.concatenate(parts, 0)
    norm = 1.0 / jnp.sqrt(1.0 + jnp.sum(degree, 1, keepdims=True))
    norm_ref[...] = jnp.broadcast_to(norm, (LOCAL_ROWS, TILE))
    pre_ref[...] = dot(feat_ref[...], ws_ref[...])


def layer_kernel(
    col_ref,
    spot_ref,
    feat_ref,
    halo_ref,
    mine_ref,
    other_ref,
    wide_ref,
    flip_ref,
    norm_ref,
    pre_ref,
    ws_ref,
    wn_ref,
    og_ref,
    act_ref,
    base_ref,
    back_ref,
    keep_ref,
    send_ref,
    table,
    gathered,
    acc,
):
    slots = flip_ref.shape[0] // TILE
    hub_tiles, column_rows, _ = mine_ref.shape
    first_hub = ROW_BLOCKS + 1
    low_core = spot_ref[0] == 0
    y, x = spot_ref[1], spot_ref[2]

    def order(tile, sign):
        down = (tile // SIDE - y) * sign & (SIDE - 1)
        along = (tile % SIDE - x) * sign & (SIDE - 1)
        down_first, along_first = down * SIDE + along, along * SIDE + down
        mine = jnp.where(low_core, down_first, along_first)
        return mine, jnp.where(low_core, along_first, down_first)

    weight_rows = D // hub_tiles

    table[:LOCAL_ROWS] = feat_ref[...]
    table[LOCAL_ROWS : LOCAL_ROWS + TILE] = halo_ref[...]

    def fill(t, carry):
        here_at, there_at = order(t, -1)
        here = mine_ref[here_at].astype(F32)
        there = other_ref[there_at].astype(F32)
        low = jnp.where(low_core, here, there)
        high = jnp.where(low_core, there, here)
        pieces = []
        for at in range(0, column_rows, OWN):
            pieces += [low[at : at + OWN], high[at : at + OWN]]
        start = pl.multiple_of((first_hub + t) * TILE, TILE)
        table[pl.ds(start, TILE)] = jnp.concatenate(pieces, 0).astype(BF16)
        return carry

    lax.fori_loop(0, hub_tiles, fill, 0)

    for s in range(slots):
        start = pl.multiple_of(col_ref[0, s] * TILE, TILE)
        gathered[s * TILE : (s + 1) * TILE] = table[pl.ds(start, TILE)]

    norm = jnp.concatenate([norm_ref[...]] * (D // TILE), 1)
    summed = dot(wide_ref[...], gathered[...])
    aggregate = (summed * norm).astype(BF16)
    own = feat_ref[...]
    preact = pre_ref[...] + dot(aggregate, wn_ref[...])
    gate = jax.nn.sigmoid(preact)
    act_ref[...] = (preact * gate).astype(BF16)
    grad_pre = (og_ref[...].astype(F32) * gate * (1.0 + preact * (1.0 - gate))).astype(BF16)
    grad_agg = (dot(grad_pre, wn_ref[...], ((1,), (1,))) * norm).astype(BF16)

    acc[...] = jnp.zeros_like(acc)
    for s in range(slots):
        into = pl.ds(pl.multiple_of(col_ref[0, s] * TILE, TILE), TILE)
        acc[into] += dot(flip_ref[s * TILE : (s + 1) * TILE], grad_agg)

    def ship(t, carry):
        start = pl.multiple_of((first_hub + t) * TILE, TILE)
        grads = acc[pl.ds(start, TILE)]
        low = jnp.concatenate([grads[at : at + OWN] for at in range(0, TILE, 2 * OWN)], 0)
        high = jnp.concatenate([grads[at + OWN : at + 2 * OWN] for at in range(0, TILE, 2 * OWN)], 0)
        keep_at, send_at = order(t, 1)
        keep_ref[keep_at, :column_rows] = jnp.where(low_core, low, high).astype(BF16)
        send_ref[send_at, :column_rows] = jnp.where(low_core, high, low).astype(BF16)
        return carry

    lax.fori_loop(0, hub_tiles, ship, 0)

    grad_self_w = dot(own, grad_pre, ((0,), (0,)))
    grad_neigh_w = dot(aggregate, grad_pre, ((0,), (0,)))
    keep = jnp.where(low_core, grad_self_w, grad_neigh_w).astype(BF16)
    send = jnp.where(low_core, grad_neigh_w, grad_self_w).astype(BF16)
    for t in range(hub_tiles):
        keep_at, send_at = order(t, 1)
        keep_ref[keep_at, column_rows:] = keep[t * weight_rows : (t + 1) * weight_rows]
        send_ref[send_at, column_rows:] = send[t * weight_rows : (t + 1) * weight_rows]
    base_ref[...] = dot(grad_pre, ws_ref[...], ((1,), (1,))) + acc[:LOCAL_ROWS]
    back_ref[...] = acc[LOCAL_ROWS : LOCAL_ROWS + TILE].astype(BF16)


SMEM = pl.BlockSpec(memory_space=pltpu.SMEM)
VMEM = pl.BlockSpec(memory_space=pltpu.VMEM)


def prepare(count, rows, adj, feat, ws):
    wide = adj.shape[0] * TILE
    return pl.pallas_call(
        prepare_kernel,
        out_shape=(
            jax.ShapeDtypeStruct((LOCAL_ROWS, wide), BF16),
            jax.ShapeDtypeStruct((wide, LOCAL_ROWS), BF16),
            jax.ShapeDtypeStruct((LOCAL_ROWS, TILE), F32),
            jax.ShapeDtypeStruct((LOCAL_ROWS, D), F32),
        ),
        in_specs=[SMEM] * 2 + [VMEM] * 3,
        out_specs=(VMEM,) * 4,
        compiler_params=pltpu.CompilerParams(vmem_limit_bytes=16 * 1024 * 1024),
        cost_estimate=pl.CostEstimate(
            flops=2 * LOCAL_ROWS * D * D, bytes_accessed=5 * 1024 * 1024, transcendentals=0
        ),
        name="prepare",
    )(count, rows, adj, feat, ws)


def layer(cols, core, feat, halo, mine, other, wide, flip, norm, pre, ws, wn, og):
    hub_tiles, column_rows, _ = mine.shape
    sources = (ROW_BLOCKS + 1 + hub_tiles) * TILE
    parcel = jax.ShapeDtypeStruct((hub_tiles, column_rows + D // hub_tiles, D), BF16)
    return pl.pallas_call(
        layer_kernel,
        out_shape=(
            jax.ShapeDtypeStruct((LOCAL_ROWS, D), BF16),
            jax.ShapeDtypeStruct((LOCAL_ROWS, D), F32),
            jax.ShapeDtypeStruct((TILE, D), BF16),
            parcel,
            parcel,
        ),
        in_specs=[SMEM] * 2 + [VMEM] * 11,
        out_specs=(VMEM,) * 5,
        scratch_shapes=[
            pltpu.VMEM((sources, D), BF16),
            pltpu.VMEM((wide.shape[1], D), BF16),
            pltpu.VMEM((sources, D), F32),
        ],
        compiler_params=pltpu.CompilerParams(vmem_limit_bytes=16 * 1024 * 1024),
        name="layer",
    )(cols, core, feat, halo, mine, other, wide, flip, norm, pre, ws, wn, og)


def swap_cores(value):
    return lax.ppermute(value, "c", [(0, 1), (1, 0)])


def ring_shift(value, steps):
    count = 1
    for axis in CHIPS:
        count *= lax.axis_size(axis)
    pairs = [(source, (source + steps) % count) for source in range(count)]
    return lax.ppermute(value, CHIPS, pairs)


def place(y, x, z, c):
    return ((y % SIDE * SIDE + x % SIDE) * ZS + z) * 2 + c


def hop(value, first, steps):
    pairs = []
    for y in range(SIDE):
        for x in range(SIDE):
            for c in (0, 1):
                down = steps if (c == 0) == first else 0
                for z in range(ZS):
                    pairs.append((place(y, x, z, c), place(y + down, x + steps - down, z, c)))
    return lax.ppermute(value, ALL, pairs)


def add_along(parts, first):
    came = [hop(parts[k], first, k) for k in (2, 1, 3)]
    total = parts[0].astype(F32)
    for part in came:
        total += part.astype(F32)
    return total.astype(BF16)


def collect(value, first):
    far, near, back = (hop(value, first, k) for k in (2, 1, 3))
    return jnp.concatenate([value, near, far, back], 0)


def exchange(value, axes):
    return lax.all_to_all(value, axes, 0, 0, tiled=True)


def spread(value, axes):
    count = math.prod(lax.axis_size(axis) for axis in axes)
    return exchange(jnp.broadcast_to(value[None], (count,) + value.shape), axes)


def per_device(
    features,
    hub_feat,
    adjacency,
    block_row,
    block_col,
    block_count,
    halo_send,
    w_self,
    w_neigh,
    out_grad,
):
    zs = lax.axis_size("z")
    planes = lax.axis_size("y") * lax.axis_size("x")
    chips = zs * planes
    core = lax.axis_index("c").astype(jnp.int32)
    picks = halo_send[0]
    chosen = (picks[:, None] == jnp.arange(LOCAL_ROWS, dtype=jnp.int32)[None, :]).astype(BF16)
    halo = ring_shift(dot(chosen, features).astype(BF16), 1)
    column = spread(hub_feat, ("z",)).reshape(zs * OWN, D)
    mine = collect(collect(column, False), True).reshape(planes, zs * OWN, D)
    mine, halo = lax.optimization_barrier((mine, halo))
    wide, flip, norm, pre = prepare(block_count, block_row, adjacency, features, w_self)
    other = swap_cores(mine)
    activations, base, back, keep, send = layer(
        block_col,
        jnp.stack([core, lax.axis_index("y"), lax.axis_index("x")]).astype(jnp.int32),
        features,
        halo,
        mine,
        other,
        wide,
        flip,
        norm,
        pre,
        w_self,
        w_neigh,
        out_grad,
    )
    returned = ring_shift(back, -1)
    chip = (keep.astype(F32) + swap_cores(send).astype(F32)).astype(BF16)
    lines = add_along(chip.reshape(SIDE, SIDE, -1, D), True)
    lines, returned = lax.optimization_barrier((lines, returned))
    plane = add_along(lines, False)
    column_rows = zs * OWN
    hub_part = plane[:column_rows].reshape(zs, OWN, D)
    weight_part = plane[column_rows:]
    packed = jnp.concatenate(
        [hub_part, jnp.broadcast_to(weight_part[None], (zs,) + weight_part.shape)], 1
    )
    total = jnp.sum(exchange(packed, ("z",)).astype(F32), 0)
    factor = 1.0 / math.sqrt(LOCAL_ROWS * 2 * chips)
    weight_mine = spread((total[OWN:] * factor).astype(BF16), PLANE).reshape(D, D)
    weight_other = swap_cores(weight_mine)
    grad_w_self = jnp.where(core == 0, weight_mine, weight_other).astype(F32)
    grad_w_neigh = jnp.where(core == 0, weight_other, weight_mine).astype(F32)
    grad_features = base + dot(chosen, returned, ((0,), (0,)))
    return (activations, grad_features, total[:OWN], grad_w_self, grad_w_neigh)


def solution(mesh):
    inner = Mesh(mesh.devices.reshape(4, 4, 8, 2), ALL)
    in_specs = (
        P(ALL, None),
        P(ALL, None),
        P(ALL, None, None),
        P(ALL, None),
        P(ALL, None),
        P(ALL),
        P(ALL, None),
        P(),
        P(),
        P(ALL, None),
    )
    out_specs = (
        P(ALL, None),
        P(ALL, None),
        P(ALL, None),
        P(),
        P(),
    )
    return jax.shard_map(
        per_device, mesh=inner, in_specs=in_specs, out_specs=out_specs, check_vma=False
    )
```

```python
import math

import jax
import jax.numpy as jnp
from jax import lax
from jax.experimental import pallas as pl
from jax.experimental.pallas import tpu as pltpu
from jax.sharding import Mesh
from jax.sharding import PartitionSpec as P

D = 512
TILE = 128
ROW_BLOCKS = 2
LOCAL_ROWS = ROW_BLOCKS * TILE
OWN = 8
F32 = jnp.float32
BF16 = jnp.bfloat16
ALL = ("y", "x", "z", "c")
CHIPS = ("y", "x", "z")
PLANE = ("y", "x")
SIDE = 4
ZS = 8


def dot(a, b, contract=((1,), (0,))):
    return lax.dot_general(a, b, (contract, ((), ())), preferred_element_type=F32)


def prepare_kernel(
    count_ref, row_ref, adj_ref, feat_ref, ws_ref, wide_ref, flip_ref, norm_ref, pre_ref
):
    slots = adj_ref.shape[0]
    count = count_ref[0]
    degree = jnp.zeros((LOCAL_ROWS, TILE), F32)
    for s in range(slots):
        span = pl.ds(s * TILE, TILE)
        tile = adj_ref[s]
        flipped = tile.T
        blank = jnp.zeros_like(tile)
        parts = []
        for r in range(ROW_BLOCKS):
            on = (row_ref[0, s] == r) & (s < count)
            part = jnp.where(on, tile, blank)
            wide_ref[r * TILE : (r + 1) * TILE, span] = part
            flip_ref[span, r * TILE : (r + 1) * TILE] = jnp.where(on, flipped, blank)
            parts.append(part.astype(F32))
        degree += jnp.concatenate(parts, 0)
    norm = 1.0 / jnp.sqrt(1.0 + jnp.sum(degree, 1, keepdims=True))
    norm_ref[...] = jnp.broadcast_to(norm, (LOCAL_ROWS, TILE))
    pre_ref[...] = dot(feat_ref[...], ws_ref[...])


def layer_kernel(
    col_ref,
    spot_ref,
    feat_ref,
    halo_ref,
    mine_ref,
    other_ref,
    wide_ref,
    flip_ref,
    norm_ref,
    pre_ref,
    ws_ref,
    wn_ref,
    og_ref,
    act_ref,
    base_ref,
    back_ref,
    keep_ref,
    send_ref,
    table,
    gathered,
    acc,
):
    slots = flip_ref.shape[0] // TILE
    hub_tiles, column_rows, _ = mine_ref.shape
    first_hub = ROW_BLOCKS + 1
    low_core = spot_ref[0] == 0
    y, x = spot_ref[1], spot_ref[2]

    def order(tile, sign):
        down = (tile // SIDE - y) * sign & (SIDE - 1)
        along = (tile % SIDE - x) * sign & (SIDE - 1)
        down_first, along_first = down * SIDE + along, along * SIDE + down
        mine = jnp.where(low_core, down_first, along_first)
        return mine, jnp.where(low_core, along_first, down_first)

    weight_rows = D // hub_tiles

    table[:LOCAL_ROWS] = feat_ref[...]
    table[LOCAL_ROWS : LOCAL_ROWS + TILE] = halo_ref[...]

    def fill(t, carry):
        here_at, there_at = order(t, -1)
        here = mine_ref[here_at].astype(F32)
        there = other_ref[there_at].astype(F32)
        low = jnp.where(low_core, here, there)
        high = jnp.where(low_core, there, here)
        pieces = []
        for at in range(0, column_rows, OWN):
            pieces += [low[at : at + OWN], high[at : at + OWN]]
        start = pl.multiple_of((first_hub + t) * TILE, TILE)
        table[pl.ds(start, TILE)] = jnp.concatenate(pieces, 0).astype(BF16)
        return carry

    lax.fori_loop(0, hub_tiles, fill, 0)

    for s in range(slots):
        start = pl.multiple_of(col_ref[0, s] * TILE, TILE)
        gathered[s * TILE : (s + 1) * TILE] = table[pl.ds(start, TILE)]

    norm = jnp.concatenate([norm_ref[...]] * (D // TILE), 1)
    summed = dot(wide_ref[...], gathered[...])
    aggregate = (summed * norm).astype(BF16)
    own = feat_ref[...]
    preact = pre_ref[...] + dot(aggregate, wn_ref[...])
    gate = jax.nn.sigmoid(preact)
    act_ref[...] = (preact * gate).astype(BF16)
    grad_pre = (og_ref[...].astype(F32) * gate * (1.0 + preact * (1.0 - gate))).astype(BF16)
    grad_agg = (dot(grad_pre, wn_ref[...], ((1,), (1,))) * norm).astype(BF16)

    acc[...] = jnp.zeros_like(acc)
    for s in range(slots):
        into = pl.ds(pl.multiple_of(col_ref[0, s] * TILE, TILE), TILE)
        acc[into] += dot(flip_ref[s * TILE : (s + 1) * TILE], grad_agg)

    def ship(t, carry):
        start = pl.multiple_of((first_hub + t) * TILE, TILE)
        grads = acc[pl.ds(start, TILE)]
        low = jnp.concatenate([grads[at : at + OWN] for at in range(0, TILE, 2 * OWN)], 0)
        high = jnp.concatenate([grads[at + OWN : at + 2 * OWN] for at in range(0, TILE, 2 * OWN)], 0)
        keep_at, send_at = order(t, 1)
        keep_ref[keep_at, :column_rows] = jnp.where(low_core, low, high).astype(BF16)
        send_ref[send_at, :column_rows] = jnp.where(low_core, high, low).astype(BF16)
        return carry

    lax.fori_loop(0, hub_tiles, ship, 0)

    grad_self_w = dot(own, grad_pre, ((0,), (0,)))
    grad_neigh_w = dot(aggregate, grad_pre, ((0,), (0,)))
    keep = jnp.where(low_core, grad_self_w, grad_neigh_w).astype(BF16)
    send = jnp.where(low_core, grad_neigh_w, grad_self_w).astype(BF16)
    for t in range(hub_tiles):
        keep_at, send_at = order(t, 1)
        keep_ref[keep_at, column_rows:] = keep[t * weight_rows : (t + 1) * weight_rows]
        send_ref[send_at, column_rows:] = send[t * weight_rows : (t + 1) * weight_rows]
    base_ref[...] = dot(grad_pre, ws_ref[...], ((1,), (1,))) + acc[:LOCAL_ROWS]
    back_ref[...] = acc[LOCAL_ROWS : LOCAL_ROWS + TILE].astype(BF16)


SMEM = pl.BlockSpec(memory_space=pltpu.SMEM)
VMEM = pl.BlockSpec(memory_space=pltpu.VMEM)


def prepare(count, rows, adj, feat, ws):
    wide = adj.shape[0] * TILE
    return pl.pallas_call(
        prepare_kernel,
        out_shape=(
            jax.ShapeDtypeStruct((LOCAL_ROWS, wide), BF16),
            jax.ShapeDtypeStruct((wide, LOCAL_ROWS), BF16),
            jax.ShapeDtypeStruct((LOCAL_ROWS, TILE), F32),
            jax.ShapeDtypeStruct((LOCAL_ROWS, D), F32),
        ),
        in_specs=[SMEM] * 2 + [VMEM] * 3,
        out_specs=(VMEM,) * 4,
        compiler_params=pltpu.CompilerParams(vmem_limit_bytes=16 * 1024 * 1024),
        cost_estimate=pl.CostEstimate(
            flops=2 * LOCAL_ROWS * D * D, bytes_accessed=5 * 1024 * 1024, transcendentals=0
        ),
        name="prepare",
    )(count, rows, adj, feat, ws)


def layer(cols, core, feat, halo, mine, other, wide, flip, norm, pre, ws, wn, og):
    hub_tiles, column_rows, _ = mine.shape
    sources = (ROW_BLOCKS + 1 + hub_tiles) * TILE
    parcel = jax.ShapeDtypeStruct((hub_tiles, column_rows + D // hub_tiles, D), BF16)
    return pl.pallas_call(
        layer_kernel,
        out_shape=(
            jax.ShapeDtypeStruct((LOCAL_ROWS, D), BF16),
            jax.ShapeDtypeStruct((LOCAL_ROWS, D), F32),
            jax.ShapeDtypeStruct((TILE, D), BF16),
            parcel,
            parcel,
        ),
        in_specs=[SMEM] * 2 + [VMEM] * 11,
        out_specs=(VMEM,) * 5,
        scratch_shapes=[
            pltpu.VMEM((sources, D), BF16),
            pltpu.VMEM((wide.shape[1], D), BF16),
            pltpu.VMEM((sources, D), F32),
        ],
        compiler_params=pltpu.CompilerParams(vmem_limit_bytes=16 * 1024 * 1024),
        name="layer",
    )(cols, core, feat, halo, mine, other, wide, flip, norm, pre, ws, wn, og)


def own_half_kernel(spot_ref, value_ref, first_ref, second_ref, wide, sem):
    wide[...] = value_ref[...].astype(F32)

    @pl.when(spot_ref[0] == 0)
    def _():
        copy = pltpu.make_async_copy(wide, first_ref, sem)
        copy.start()
        copy.wait()

    @pl.when(spot_ref[0] != 0)
    def _():
        copy = pltpu.make_async_copy(wide, second_ref, sem)
        copy.start()
        copy.wait()


def other_half_kernel(spot_ref, value_ref, first_in, second_in, first_ref, second_ref, wide, sem):
    del first_in, second_in
    wide[...] = value_ref[...].astype(F32)

    @pl.when(spot_ref[0] != 0)
    def _():
        copy = pltpu.make_async_copy(wide, first_ref, sem)
        copy.start()
        copy.wait()

    @pl.when(spot_ref[0] == 0)
    def _():
        copy = pltpu.make_async_copy(wide, second_ref, sem)
        copy.start()
        copy.wait()


def write_half(spot, value, pair):
    anywhere = pl.BlockSpec(memory_space=pl.ANY)
    full = jax.ShapeDtypeStruct(value.shape, F32)
    return pl.pallas_call(
        other_half_kernel if pair else own_half_kernel,
        out_shape=(full, full),
        in_specs=[SMEM, VMEM] + [anywhere] * len(pair),
        out_specs=(anywhere, anywhere),
        scratch_shapes=[pltpu.VMEM(value.shape, F32), pltpu.SemaphoreType.DMA],
        input_output_aliases={2: 0, 3: 1} if pair else {},
        compiler_params=pltpu.CompilerParams(vmem_limit_bytes=16 * 1024 * 1024),
        name="other_half" if pair else "own_half",
    )(spot, value, *pair)


def swap_cores(value):
    return lax.ppermute(value, "c", [(0, 1), (1, 0)])


def ring_shift(value, steps):
    count = 1
    for axis in CHIPS:
        count *= lax.axis_size(axis)
    pairs = [(source, (source + steps) % count) for source in range(count)]
    return lax.ppermute(value, CHIPS, pairs)


def place(y, x, z, c):
    return ((y % SIDE * SIDE + x % SIDE) * ZS + z) * 2 + c


def hop(value, first, steps):
    pairs = []
    for y in range(SIDE):
        for x in range(SIDE):
            for c in (0, 1):
                down = steps if (c == 0) == first else 0
                for z in range(ZS):
                    pairs.append((place(y, x, z, c), place(y + down, x + steps - down, z, c)))
    return lax.ppermute(value, ALL, pairs)


def add_along(parts, first):
    came = [hop(parts[k], first, k) for k in (2, 1, 3)]
    total = parts[0].astype(F32)
    for part in came:
        total += part.astype(F32)
    return total.astype(BF16)


def collect(value, first):
    far, near, back = (hop(value, first, k) for k in (2, 1, 3))
    return jnp.concatenate([value, near, far, back], 0)


def exchange(value, axes):
    return lax.all_to_all(value, axes, 0, 0, tiled=True)


def spread(value, axes):
    count = math.prod(lax.axis_size(axis) for axis in axes)
    return exchange(jnp.broadcast_to(value[None], (count,) + value.shape), axes)


def per_device(
    features,
    hub_feat,
    adjacency,
    block_row,
    block_col,
    block_count,
    halo_send,
    w_self,
    w_neigh,
    out_grad,
):
    zs = lax.axis_size("z")
    planes = lax.axis_size("y") * lax.axis_size("x")
    chips = zs * planes
    core = lax.axis_index("c").astype(jnp.int32)
    picks = halo_send[0]
    chosen = (picks[:, None] == jnp.arange(LOCAL_ROWS, dtype=jnp.int32)[None, :]).astype(BF16)
    halo = ring_shift(dot(chosen, features).astype(BF16), 1)
    column = spread(hub_feat, ("z",)).reshape(zs * OWN, D)
    mine = collect(collect(column, False), True).reshape(planes, zs * OWN, D)
    mine, halo = lax.optimization_barrier((mine, halo))
    wide, flip, norm, pre = prepare(block_count, block_row, adjacency, features, w_self)
    other = swap_cores(mine)
    activations, base, back, keep, send = layer(
        block_col,
        jnp.stack([core, lax.axis_index("y"), lax.axis_index("x")]).astype(jnp.int32),
        features,
        halo,
        mine,
        other,
        wide,
        flip,
        norm,
        pre,
        w_self,
        w_neigh,
        out_grad,
    )
    returned = ring_shift(back, -1)
    chip = (keep.astype(F32) + swap_cores(send).astype(F32)).astype(BF16)
    lines = add_along(chip.reshape(SIDE, SIDE, -1, D), True)
    lines, returned = lax.optimization_barrier((lines, returned))
    grad_features = base + dot(chosen, returned, ((0,), (0,)))
    plane = add_along(lines, False)
    plane, grad_features = lax.optimization_barrier((plane, grad_features))
    column_rows = zs * OWN
    hub_part = plane[:column_rows].reshape(zs, OWN, D)
    weight_part = plane[column_rows:]
    packed = jnp.concatenate(
        [hub_part, jnp.broadcast_to(weight_part[None], (zs,) + weight_part.shape)], 1
    )
    total = jnp.sum(exchange(packed, ("z",)).astype(F32), 0)
    factor = 1.0 / math.sqrt(LOCAL_ROWS * 2 * chips)
    weight_mine = spread((total[OWN:] * factor).astype(BF16), PLANE).reshape(D, D)
    weight_other = swap_cores(weight_mine)
    halves = write_half(core.reshape(1), weight_mine, ())
    grad_w_self, grad_w_neigh = write_half(core.reshape(1), weight_other, halves)
    return (activations, grad_features, total[:OWN], grad_w_self, grad_w_neigh)


def solution(mesh):
    inner = Mesh(mesh.devices.reshape(4, 4, 8, 2), ALL)
    in_specs = (
        P(ALL, None),
        P(ALL, None),
        P(ALL, None, None),
        P(ALL, None),
        P(ALL, None),
        P(ALL),
        P(ALL, None),
        P(),
        P(),
        P(ALL, None),
    )
    out_specs = (
        P(ALL, None),
        P(ALL, None),
        P(ALL, None),
        P(),
        P(),
    )
    return jax.shard_map(
        per_device, mesh=inner, in_specs=in_specs, out_specs=out_specs, check_vma=False
    )
```
